512 devices in a mesh: pos: 32 (over y_hi, x, core), chan: 16 (over y_lo, z).
Axes of the slice: x: 4, y: 8 (y_hi: 4, y_lo: 2; y = y_hi * 2 + y_lo), z: 8, core: 2. Of those that a mesh axis runs over, the one named last changes fastest.
Arguments:
- q_in: bfloat16 [4096, 8192], P('pos', 'chan'), may hold values from -6 to 6
- k_in: bfloat16 [4096, 8192], P('pos', 'chan'), may hold values from -6 to 6
- v_in: bfloat16 [4096, 8192], P('pos', 'chan'), may hold values from -6 to 6
- short_weights: float32 [3, 3, 8192], P(None, None, 'chan'), may hold values from -3 to 3
- residues: float32 [8192, 16], P('chan')
- log_decay: float32 [8192, 16], P('chan')
- out_weight: bfloat16 [8192, 8192], P('chan', 'pos'), may hold values from -0.0625 to 0.0625
- grad_out: bfloat16 [4096, 8192], P(('pos', 'chan')), may hold values from -6 to 6
Outputs:
- grad_q: bfloat16 [4096, 8192], P('pos', 'chan')
- grad_k: bfloat16 [4096, 8192], P('pos', 'chan')
- grad_v: bfloat16 [4096, 8192], P('pos', 'chan')
- grad_short: float32 [3, 3, 8192], P(None, None, 'chan')
- grad_residues: float32 [8192, 16], P('chan')
- grad_log_decay: float32 [8192, 16], P('chan')
The draws below stay inside these ranges and needn't reach their ends.
All inputs are finite; a program needn't handle non-finite values.
Results may differ from the reference program's by a relative error of at most 0.029.
Values may be sent and summed in bfloat16 or wider, within the bound.
A program may use at most 64 MiB of HBM per device.

```python
import math
import jax
import jax.numpy as jnp
from jax import lax

D = 8192
NS = 16
KS = 3
SEQ = 4096


def decay_law(key, lower, upper):
    return jax.random.uniform(key, (D, NS), jnp.float32, lower, upper)


def draw_log_decay(key, part):
    return decay_law(key, math.log(0.5 / SEQ), math.log(0.1))


def draw_residues(key, part):
    theta = decay_law(key, math.log(0.5 / SEQ), math.log(0.1))
    key = jax.random.fold_in(key, 7)
    return jax.random.normal(key, (D, NS), jnp.float32) * jnp.sqrt(2.0 * jnp.exp(theta) / NS)


def block_scale(own_key, shape, split, least, high):
    loudness = 1.0
    for dim, blocks in split:
        heights = jax.random.uniform(jax.random.fold_in(jax.random.fold_in(own_key, 6), dim), (blocks,), jnp.float32, least / len(split), high / len(split))
        loudness = loudness * jnp.repeat(jnp.exp(heights), shape[dim] // blocks).reshape((-1,) + (1,) * (len(shape) - 1 - dim))
    return loudness


def noise(stream_key, dims, scale, bound, cuts=(), held_as=jnp.bfloat16):
    values = scale * jax.random.normal(stream_key, dims, jnp.float32)
    if cuts:
        values = values * block_scale(stream_key, dims, cuts, -0.22, 0.18)
    return jnp.clip(values, -bound, bound).astype(held_as)


def setup_inputs(seed: int = 0) -> dict:
    streams_of = jax.random.split(jax.random.key(seed), 9)
    return {
        "q_in": noise(streams_of[0], (SEQ, D), 1.0, 6.0, ((0, 32), (1, 16))),
        "k_in": noise(streams_of[1], (SEQ, D), 1.0, 6.0, ((0, 32), (1, 16))),
        "v_in": noise(streams_of[2], (SEQ, D), 1.0, 6.0, ((0, 32), (1, 16))),
        "short_weights": noise(streams_of[3], (3, KS, D), 0.6, 3.0, ((2, 16),), jnp.float32),
        "residues": draw_residues(jax.random.fold_in(streams_of[8], 71), 0),
        "log_decay": draw_log_decay(jax.random.fold_in(streams_of[8], 71), 0),
        "out_weight": noise(streams_of[6], (D, D), D ** -0.5, 0.0625, ((0, 16), (1, 32))),
        "grad_out": noise(streams_of[7], (SEQ, D), 1.0, 6.0, ((0, 512),)),
    }


def filter_taps(residue, rate, times):
    def per_mode(accum, pair):
        weight, decay = pair
        return accum + weight[:, None] * jnp.exp(-decay[:, None] * times[None, :]), None
    start = jnp.zeros((residue.shape[0], times.shape[0]), jnp.float32)
    taps, _ = lax.scan(per_mode, start, (residue.T, rate.T))
    return taps


def mode_sums(grad_taps, residue, rate, times):
    def per_mode(accum, pair):
        weight, decay = pair
        falloff = jnp.exp(-decay[:, None] * times[None, :])
        first = jnp.sum(grad_taps * falloff, axis=1)
        second = -jnp.sum(grad_taps * (times[None, :] * falloff), axis=1) * weight * decay
        return accum, (first, second)
    _, (by_residue, by_rate) = lax.scan(per_mode, jnp.zeros((), jnp.float32), (residue.T, rate.T))
    return by_residue.T, by_rate.T


def block_grads(streams, weights, residue, log_rate, out_rows, cotangent):
    taps_count = weights.shape[1]
    padded = jnp.pad(streams.astype(jnp.float32), ((0, 0), (0, 0), (taps_count - 1, 0)))
    conv = sum(weights[:, lag, :, None] * padded[:, :, taps_count - 1 - lag: taps_count - 1 - lag + SEQ]
               for lag in range(taps_count))
    q_conv = conv[0].astype(jnp.bfloat16)
    k_conv = conv[1]
    v_conv = conv[2]
    gated = (k_conv * v_conv).astype(jnp.bfloat16)
    grad_mix = jnp.dot(out_rows, cotangent.T, preferred_element_type=jnp.float32).astype(jnp.bfloat16)
    rate = jnp.exp(log_rate)
    times = jnp.arange(SEQ).astype(jnp.float32)
    taps = filter_taps(residue, rate, times)
    length = 2 * SEQ
    taps_hat = jnp.fft.fft(taps, n=length, axis=1)
    gated_hat = jnp.fft.fft(gated.astype(jnp.float32), n=length, axis=1)
    filtered = jnp.real(jnp.fft.ifft(taps_hat * gated_hat, axis=1))[:, :SEQ]
    mix = grad_mix.astype(jnp.float32)
    grad_q_conv = mix * filtered
    grad_filtered = (mix * q_conv.astype(jnp.float32)).astype(jnp.bfloat16)
    grad_hat = jnp.fft.fft(grad_filtered.astype(jnp.float32), n=length, axis=1)
    grad_gated = jnp.real(jnp.fft.ifft(jnp.conj(taps_hat) * grad_hat, axis=1))[:, :SEQ]
    grad_taps = jnp.real(jnp.fft.ifft(grad_hat * jnp.conj(gated_hat), axis=1))[:, :SEQ]
    grad_streams = jnp.stack([grad_q_conv, grad_gated * v_conv, grad_gated * k_conv])
    padded_grad = jnp.pad(grad_streams, ((0, 0), (0, 0), (0, taps_count - 1)))
    grad_inputs = sum(weights[:, lag, :, None] * padded_grad[:, :, lag: lag + SEQ]
                      for lag in range(taps_count)).astype(jnp.bfloat16)
    grad_weights = jnp.stack([jnp.sum(grad_streams * padded[:, :, taps_count - 1 - lag: taps_count - 1 - lag + SEQ], axis=2)
                              for lag in range(taps_count)], axis=1)
    by_residue, by_rate = mode_sums(grad_taps, residue, rate, times)
    return grad_inputs, grad_weights, by_residue, by_rate


def reference(q_in, k_in, v_in, short_weights, residues, log_decay, out_weight, grad_out):
    blocks = 16
    block_width = D // blocks
    streams = jnp.stack([q_in, k_in, v_in]).reshape(3, SEQ, blocks, block_width).transpose(2, 0, 3, 1)
    weights = short_weights.reshape(3, KS, blocks, block_width).transpose(2, 0, 1, 3)
    block_residues = residues.reshape(blocks, block_width, NS)
    block_rates = log_decay.reshape(blocks, block_width, NS)
    block_rows = out_weight.reshape(blocks, block_width, D)

    def one_block(items):
        return block_grads(items[0], items[1], items[2], items[3], items[4], grad_out)

    grad_inputs, grad_weights, by_residue, by_rate = lax.map(
        one_block, (streams, weights, block_residues, block_rates, block_rows))
    grad_inputs = grad_inputs.transpose(1, 3, 0, 2).reshape(3, SEQ, D)
    grad_short = grad_weights.transpose(1, 2, 0, 3).reshape(3, KS, D)
    return (grad_inputs[0], grad_inputs[1], grad_inputs[2], grad_short,
            by_residue.reshape(D, NS), by_rate.reshape(D, NS))
```

```python
import functools

import jax
import jax.numpy as jnp
from jax import lax
from jax.experimental import pallas as pl
from jax.experimental.pallas import tpu as pltpu
from jax.sharding import PartitionSpec as P

F32 = jnp.float32
BF16 = jnp.bfloat16
MESH = pl.DeviceIdType.MESH

YH, XN, CORES = 4, 4, 2
YL, ZN = 2, 8
POS = YH * XN * CORES
CHAN = YL * ZN
ROW = XN * CORES
BLK = 128
OWN = 16
MODES = 16
TAPS = 3


def remote(src, dst, send, recv, **device):
    return pltpu.make_async_remote_copy(
        src_ref=src, dst_ref=dst, send_sem=send, recv_sem=recv,
        device_id=device, device_id_type=MESH,
    )


def full(memory=pltpu.VMEM):
    return pl.BlockSpec(memory_space=memory)


def later(x, j):
    if j == 0:
        return x
    lane = lax.broadcasted_iota(jnp.int32, x.shape, 2)
    turned = pltpu.roll(x, j, 2)
    before = jnp.concatenate([jnp.zeros_like(turned[:1]), turned[:-1]], axis=0)
    return jnp.where(lane < j, before, turned)


def sooner(x, j):
    if j == 0:
        return x
    lane = lax.broadcasted_iota(jnp.int32, x.shape, 2)
    turned = pltpu.roll(x, BLK - j, 2)
    after = jnp.concatenate([turned[1:], jnp.zeros_like(turned[:1])], axis=0)
    return jnp.where(lane >= BLK - j, after, turned)


def halves(x):
    high = x.astype(BF16)
    return high, (x - high.astype(F32)).astype(BF16)


def dot(a, b, da, db):
    return lax.dot_general(a, b, (((da,), (db,)), ((), ())), preferred_element_type=F32)


def mixer_kernel(qkv, gm, sw, res, ld, out, small, xs, xr, gs, fs, gg, up, vp, cd):
    me = lax.axis_index("pos")
    first = me * OWN
    chans = sw.shape[2]
    pick = lax.broadcasted_iota(jnp.int32, (OWN, chans), 1) == (
        first + lax.broadcasted_iota(jnp.int32, (OWN, chans), 0)
    )
    cols = [
        [
            jnp.sum(jnp.where(pick, sw[s, pl.ds(j, 1), :], 0.0), axis=1, keepdims=True)[None]
            for j in range(TAPS)
        ]
        for s in range(3)
    ]
    streams = [qkv[:, s].astype(F32) for s in range(3)]

    def conv(s):
        return sum(cols[s][j] * later(streams[s], j) for j in range(TAPS))

    kc, vc = conv(1), conv(2)
    rows = qkv.shape[0] * OWN
    gated = (kc * vc).astype(BF16)
    xs[...] = gated.astype(F32).reshape(rows, BLK)
    mix = gm[...].astype(F32)
    gs[...] = (mix * conv(0).astype(BF16).astype(F32)).astype(BF16).astype(F32).reshape(rows, BLK)
    flip = (
        lax.broadcasted_iota(jnp.int32, (BLK, BLK), 0)
        + lax.broadcasted_iota(jnp.int32, (BLK, BLK), 1)
        == BLK - 1
    ).astype(F32).astype(BF16)
    xr[...] = dot(xs[...].astype(BF16), flip, 1, 0)

    eye = (
        lax.broadcasted_iota(jnp.int32, (OWN, MODES, MODES), 1)
        == lax.broadcasted_iota(jnp.int32, (OWN, MODES, MODES), 2)
    )

    def columns(ref):
        own = ref[pl.ds(pl.multiple_of(first, OWN), OWN), :]
        spread = jnp.where(eye, jnp.broadcast_to(own[:, None, :], eye.shape), 0.0)
        return jnp.sum(spread, axis=2, keepdims=True)

    shape3 = (OWN, MODES, BLK)
    time = lax.broadcasted_iota(jnp.int32, shape3, 2).astype(F32)
    weight = jnp.broadcast_to(columns(res), shape3)
    rate = jnp.exp(jnp.broadcast_to(columns(ld), shape3))
    near = jnp.exp(-rate * time)
    ahead = jnp.exp(-rate * (time + 1.0))
    back = jnp.exp(-rate * (BLK - 1.0 - time))
    taps = jnp.sum(weight * near, axis=1)
    t_ahead = (time + 1.0) * ahead
    t_back = (BLK - 1.0 - time) * back
    w_ahead = weight * ahead
    w_back = weight * back

    row2 = lax.broadcasted_iota(jnp.int32, (BLK, BLK), 0)
    lane2 = lax.broadcasted_iota(jnp.int32, (BLK, BLK), 1)
    blocks = qkv.shape[0]
    fill = jnp.zeros((BLK - blocks, BLK), F32)
    for c in range(OWN):
        own = pl.ds(c, blocks, stride=OWN)
        x = xs[own, :]
        g = gs[own, :]
        xb, gb = x.astype(BF16), g.astype(BF16)
        spread = pltpu.roll(
            jnp.broadcast_to(taps[c : c + 1], (BLK, BLK)), 0, 1, stride=1, stride_axis=0
        )
        toeplitz = jnp.where(lane2 >= row2, spread, 0.0).astype(BF16)
        here = pl.ds(c * blocks, blocks)
        fs[here, :] = dot(xb, toeplitz, 1, 0)
        gg[here, :] = dot(gb, toeplitz, 1, 1)
        pair = dot(xr[own, :].astype(BF16), gb, 0, 0)
        turned = pltpu.roll(pair, 1, 1, stride=1, stride_axis=0)
        cd[pl.ds(c, 1), :] = jnp.sum(jnp.where(lane2 <= row2, turned, 0.0), axis=0, keepdims=True)
        xw = jnp.concatenate([x, fill], axis=0).astype(BF16)
        gw = jnp.concatenate([g, fill], axis=0).astype(BF16)
        left = jnp.concatenate([*halves(back[c]), *halves(t_back[c])], axis=0)
        right = jnp.concatenate([*halves(ahead[c]), *halves(t_ahead[c])], axis=0)
        up[c] = dot(left, xw, 1, 1)
        vp[c] = dot(right, gw, 1, 1)

    n = MODES
    s0, s1 = up[:, 0:n] + up[:, n : 2 * n], up[:, 2 * n : 3 * n] + up[:, 3 * n : 4 * n]
    t0, t1 = vp[:, 0:n] + vp[:, n : 2 * n], vp[:, 2 * n : 3 * n] + vp[:, 3 * n : 4 * n]
    rest = t0
    for k in (1, 2, 4, 8, 16):
        fall = jnp.exp(-rate * float(BLK * k))
        s0_k = pltpu.roll(s0, k, 2)
        s1 = s1 + fall * (pltpu.roll(s1, k, 2) + float(BLK * k) * s0_k)
        s0 = s0 + fall * s0_k
        rest = rest + fall * pltpu.roll(rest, BLK - k, 2)
    state, d_state = pltpu.roll(s0, 1, 2), pltpu.roll(s1, 1, 2)
    rest = pltpu.roll(rest, BLK - 1, 2)
    corr = cd[...][:, None, :] * near
    by_res = jnp.sum(corr + t0 * state, axis=2, keepdims=True)
    by_rate = jnp.sum(corr * time + t1 * state + t0 * d_state, axis=2, keepdims=True)
    by_log = -by_rate * weight * rate
    lane3 = lax.broadcasted_iota(jnp.int32, shape3, 2)
    mode3 = lax.broadcasted_iota(jnp.int32, shape3, 1)
    tiny = jnp.sum(
        jnp.where(lane3 == 16 + mode3, by_res, jnp.where(lane3 == 32 + mode3, by_log, 0.0)), axis=1
    )

    for c in range(OWN):
        own = pl.ds(c, blocks, stride=OWN)
        here = pl.ds(c * blocks, blocks)

        def joined(states, table):
            sh, sl = halves(states)
            th, tl = halves(table)
            a = jnp.concatenate([sh, sh, sl], axis=0)
            b = jnp.concatenate([th, tl, th], axis=0)
            return dot(a, b, 0, 0)[:blocks]

        xs[own, :] = fs[here, :] + joined(state[c], w_ahead[c])
        gs[own, :] = gg[here, :] + joined(rest[c], w_back[c])

    shape = (blocks, OWN, BLK)
    grad_gated = gs[...].reshape(shape)
    grads = (mix * xs[...].reshape(shape), grad_gated * vc, grad_gated * kc)
    lane = lax.broadcasted_iota(jnp.int32, (OWN, BLK), 1)
    for s in range(3):
        out[:, s] = sum(cols[s][j] * sooner(grads[s], j) for j in range(TAPS)).astype(BF16)
        for j in range(TAPS):
            total = jnp.sum(jnp.sum(grads[s] * later(streams[s], j), axis=0), axis=1, keepdims=True)
            tiny = jnp.where(lane == s * TAPS + j, total, tiny)
    small[...] = tiny


def mixer(qkv, gm, short_weights, residues, log_decay):
    blocks = qkv.shape[0]
    rows = blocks * OWN
    return pl.pallas_call(
        mixer_kernel,
        out_shape=(
            jax.ShapeDtypeStruct((blocks, 3, OWN, BLK), BF16),
            jax.ShapeDtypeStruct((OWN, BLK), F32),
        ),
        in_specs=[full()] * 5,
        out_specs=(full(), full()),
        scratch_shapes=[pltpu.VMEM((rows, BLK), F32)] * 5
        + [pltpu.VMEM((OWN, 4 * MODES, BLK), F32)] * 2
        + [pltpu.VMEM((OWN, BLK), F32)],
        compiler_params=pltpu.CompilerParams(vmem_limit_bytes=48 * 1024 * 1024),
        name="mixer",
    )(qkv, gm, short_weights, residues, log_decay)


def gather_kernel(q, k, v, w, g, qkv_out, gm_out, slab, inb, wbuf, gst, xbuf, pout, pin,
                  qs, qr, gss, gsr, ws, wr, ls, lr, rs, rr, ps, pr):
    p = lax.axis_index("pos")
    c = lax.axis_index("chan")
    h, x, core = p // ROW, (p // CORES) % XN, p % CORES
    l, z = c // ZN, c % ZN
    other = (1 - l) * ZN + z
    up, down = l * ZN + (z + 1) % ZN, l * ZN + (z + ZN - 1) % ZN
    sibling = p + 1 - 2 * core

    barrier = pltpu.get_barrier_semaphore()

    @pl.loop(1, POS)
    def _(i):
        pl.semaphore_signal(barrier, 1, device_id={"pos": (p + i) % POS}, device_id_type=MESH)

    for d in (other, up, down):
        pl.semaphore_signal(barrier, 1, device_id={"chan": d}, device_id_type=MESH)

    wide = g[...].astype(F32)
    part = wide.shape[1] // YH
    for i in range(YH):
        at = i * part
        gst[i] = jnp.concatenate(
            [wide[:, at : at + part // 2], wide[:, at + part // 2 : at + part]], axis=0
        ).astype(BF16)
    pl.semaphore_wait(barrier, POS - 1 + 3)

    first = []
    for i in range(1, YH):
        to = (h + i) % YH
        first.append(remote(gst.at[to], xbuf.at[c, h], gss.at[i - 1], gsr.at[i - 1],
                            pos=to * ROW + x * CORES + core))
        first[-1].start()
    mine = x * CORES + core
    cols = w.shape[1]

    def wcols(slot):
        return wbuf.at[:, pl.ds(pl.multiple_of(slot * cols, cols), cols)]

    weights = []
    for i in (1, 3, 2):
        to = h * ROW + ((x + i) % XN) * CORES + core
        weights.append(remote(w, wcols(mine), ws.at[i - 1], wr.at[i - 1], pos=to))
        weights[-1].start()
    share = remote(w, wcols(mine), ws.at[3], wr.at[3], pos=sibling)
    share.start()
    xbuf[c, h] = gst[h]

    for s, ref in enumerate((q, k, v)):
        slab[:, s] = ref[...].astype(F32).T.astype(BF16).reshape(POS, OWN, BLK)

    for i, copy in enumerate(first):
        copy.wait_recv()
    across = remote(xbuf.at[c], xbuf.at[c], ls, lr, chan=other)
    across.start()

    def ring(way, sel, step):
        chip = (z - (step - 1) + ZN) % ZN if way == 0 else (z + step - 1) % ZN
        slot = (l if sel == 0 else 1 - l) * ZN + chip
        sem = (way * 2 + sel) * 4 + step - 1
        return remote(xbuf.at[slot], xbuf.at[slot], rs.at[sem], rr.at[sem],
                      chan=up if way == 0 else down)

    hops = []

    def send(way, sel, step):
        hops.append(ring(way, sel, step))
        hops[-1].start()

    send(0, 0, 1)
    send(1, 0, 1)

    @pl.loop(1, POS)
    def _(i):
        to = (p + i) % POS
        remote(slab.at[to], inb.at[p], qs.at[i], qr.at[i], pos=to).start()

    inb[p] = slab[p]
    wcols(mine)[...] = w[...]

    across.wait_recv()
    send(0, 1, 1)
    send(1, 1, 1)

    shared = []

    def share_weights(i):
        slot = ((x + XN - i) % XN) * CORES + core
        remote(w, wcols(slot), ws.at[i - 1], wr.at[i - 1], pos=sibling).wait_recv()
        shared.append(remote(wcols(slot), wcols(slot), ws.at[3 + i], wr.at[3 + i], pos=sibling))
        shared[-1].start()

    for step in range(1, ZN // 2 + 1):
        for sel in (0, 1):
            for way in (0, 1):
                if step == ZN // 2 and way != sel:
                    continue
                ring(way, sel, step).wait_recv()
                if step + 1 < ZN // 2 or (step + 1 == ZN // 2 and way == sel):
                    send(way, sel, step + 1)
        if step == 1:
            share_weights(1)
            share_weights(3)
        if step == 2:
            share_weights(2)
    share.wait_recv()
    for copy in shared:
        copy.wait_recv()

    half = xbuf.shape[3]
    for i in range(0, YH, 2):
        tiles = []
        for j in (i, i + 1):
            both = xbuf[:, j].astype(F32).reshape(CHAN, 2, 8, half)
            tiles.append(
                jnp.concatenate([both[:, 0].reshape(BLK, half), both[:, 1].reshape(BLK, half)], axis=1)
            )
        rows = jnp.concatenate(tiles, axis=0).astype(BF16)
        part = lax.dot_general(
            wbuf[...], rows, (((1,), (1,)), ((), ())), preferred_element_type=F32
        ).astype(BF16)
        pout[:, i] = part[:, :BLK].reshape(POS, OWN, BLK)
        pout[:, i + 1] = part[:, BLK:].reshape(POS, OWN, BLK)

    @pl.loop(1, POS)
    def _(i):
        to = (p + i) % POS
        remote(pout.at[to], pin.at[p], ps.at[i], pr.at[i], pos=to).start()

    pin[p] = pout[p]

    @pl.loop(1, POS)
    def _(i):
        at = (p + POS - i) % POS
        remote(slab.at[at], inb.at[at], qs.at[i], qr.at[i], pos=at).wait()

    qkv_out[...] = inb[...]

    @pl.loop(1, POS)
    def _(i):
        at = (p + POS - i) % POS
        remote(pout.at[at], pin.at[at], ps.at[i], pr.at[i], pos=at).wait()

    for i in range(YH):
        total = sum(pin[pl.ds(j * ROW, ROW), i].astype(F32) for j in range(YH))
        gm_out[pl.ds(i * ROW, ROW)] = total.astype(BF16)

    for copy in first + weights + [share, across] + hops + shared:
        copy.wait_send()


def gather(q, k, v, w, g):
    chans, cols = w.shape
    dma = pltpu.SemaphoreType.DMA
    half = g.shape[1] // YH // 2
    return pl.pallas_call(
        gather_kernel,
        out_shape=(
            jax.ShapeDtypeStruct((POS, 3, OWN, BLK), BF16),
            jax.ShapeDtypeStruct((POS, OWN, BLK), BF16),
        ),
        in_specs=[full()] * 5,
        out_specs=(full(), full()),
        scratch_shapes=[
            pltpu.VMEM((POS, 3, OWN, BLK), BF16),
            pltpu.VMEM((POS, 3, OWN, BLK), BF16),
            pltpu.VMEM((chans, ROW * cols), BF16),
            pltpu.VMEM((YH, 16, half), BF16),
            pltpu.VMEM((CHAN, YH, 16, half), BF16),
            pltpu.VMEM((POS, YH, OWN, BLK), BF16),
            pltpu.VMEM((POS, YH, OWN, BLK), BF16),
            dma((POS,)), dma((POS,)),
            dma((YH - 1,)), dma((YH - 1,)),
            dma((7,)), dma((7,)),
            dma, dma,
            dma((16,)), dma((16,)),
            dma((POS,)), dma((POS,)),
        ],
        compiler_params=pltpu.CompilerParams(
            collective_id=0, has_side_effects=True, vmem_limit_bytes=48 * 1024 * 1024
        ),
        name="gather",
    )(q, k, v, w, g)


def spread_kernel(gin, small, gout, sout, gb, sb, gs, gr, ss, sr):
    p = lax.axis_index("pos")
    barrier = pltpu.get_barrier_semaphore()

    @pl.loop(1, POS)
    def _(i):
        pl.semaphore_signal(barrier, 1, device_id={"pos": (p + i) % POS}, device_id_type=MESH)

    pl.semaphore_wait(barrier, POS - 1)

    @pl.loop(1, POS)
    def _(i):
        to = (p + i) % POS
        remote(gin.at[to], gb.at[p], gs.at[i], gr.at[i], pos=to).start()
        remote(small, sb.at[p], ss.at[i], sr.at[i], pos=to).start()

    gb[p] = gin[p]
    sb[p] = small[...]

    @pl.loop(1, POS)
    def _(i):
        at = (p + POS - i) % POS
        remote(gin.at[at], gb.at[at], gs.at[i], gr.at[i], pos=at).wait()
        remote(small, sb.at[at], ss.at[i], sr.at[i], pos=at).wait()

    gout[...] = gb[...]
    sout[...] = sb[...]


def spread(grads, small):
    dma = pltpu.SemaphoreType.DMA
    return pl.pallas_call(
        spread_kernel,
        out_shape=(
            jax.ShapeDtypeStruct((POS, 3, OWN, BLK), BF16),
            jax.ShapeDtypeStruct((POS, OWN, BLK), F32),
        ),
        in_specs=[full()] * 2,
        out_specs=(full(), full()),
        scratch_shapes=[
            pltpu.VMEM((POS, 3, OWN, BLK), BF16),
            pltpu.VMEM((POS, OWN, BLK), F32),
            dma((POS,)), dma((POS,)), dma((POS,)), dma((POS,)),
        ],
        compiler_params=pltpu.CompilerParams(
            collective_id=1, has_side_effects=True, vmem_limit_bytes=48 * 1024 * 1024
        ),
        name="spread",
    )(grads, small)


def finish_kernel(gin, small, q, k, v, short, res, dec):
    chans = POS * OWN
    for s, ref in enumerate((q, k, v)):
        ref[...] = gin[:, s].astype(F32).reshape(chans, BLK).T.astype(BF16)
    tiny = small[...].reshape(chans, BLK)
    res[...] = tiny[:, 16:32]
    dec[...] = tiny[:, 32:48]
    turned = tiny.T
    for s in range(3):
        short[s] = turned[s * TAPS : (s + 1) * TAPS]


def finish(grads, small):
    chans = POS * OWN
    stream = jax.ShapeDtypeStruct((BLK, chans), BF16)
    mode = jax.ShapeDtypeStruct((chans, MODES), F32)
    return pl.pallas_call(
        finish_kernel,
        out_shape=(stream, stream, stream, jax.ShapeDtypeStruct((3, TAPS, chans), F32), mode, mode),
        in_specs=[full()] * 2,
        out_specs=(full(),) * 6,
        compiler_params=pltpu.CompilerParams(vmem_limit_bytes=48 * 1024 * 1024),
        name="finish",
    )(grads, small)


def local(q_in, k_in, v_in, short_weights, residues, log_decay, out_weight, grad_out):
    qkv, gm = gather(q_in, k_in, v_in, out_weight, grad_out)
    grads, small = mixer(qkv, gm, short_weights, residues, log_decay)
    return finish(*spread(grads, small))


def solution(mesh):
    in_specs = (
        P("pos", "chan"),
        P("pos", "chan"),
        P("pos", "chan"),
        P(None, None, "chan"),
        P("chan", None),
        P("chan", None),
        P("chan", "pos"),
        P(("pos", "chan"), None),
    )
    out_specs = (
        P("pos", "chan"),
        P("pos", "chan"),
        P("pos", "chan"),
        P(None, None, "chan"),
        P("chan", None),
        P("chan", None),
    )
    return jax.shard_map(local, mesh=mesh, in_specs=in_specs, out_specs=out_specs, check_vma=False)
```

```python
import functools

import jax
import jax.numpy as jnp
from jax import lax
from jax.experimental import pallas as pl
from jax.experimental.pallas import tpu as pltpu
from jax.sharding import PartitionSpec as P

F32 = jnp.float32
BF16 = jnp.bfloat16
MESH = pl.DeviceIdType.MESH

YH, XN, CORES = 4, 4, 2
YL, ZN = 2, 8
POS = YH * XN * CORES
CHAN = YL * ZN
ROW = XN * CORES
BLK = 128
OWN = 16
MODES = 16
TAPS = 3


def remote(src, dst, send, recv, **device):
    return pltpu.make_async_remote_copy(
        src_ref=src, dst_ref=dst, send_sem=send, recv_sem=recv,
        device_id=device, device_id_type=MESH,
    )


def full(memory=pltpu.VMEM):
    return pl.BlockSpec(memory_space=memory)


def later(x, j):
    if j == 0:
        return x
    lane = lax.broadcasted_iota(jnp.int32, x.shape, 2)
    turned = pltpu.roll(x, j, 2)
    before = jnp.concatenate([jnp.zeros_like(turned[:1]), turned[:-1]], axis=0)
    return jnp.where(lane < j, before, turned)


def sooner(x, j):
    if j == 0:
        return x
    lane = lax.broadcasted_iota(jnp.int32, x.shape, 2)
    turned = pltpu.roll(x, BLK - j, 2)
    after = jnp.concatenate([turned[1:], jnp.zeros_like(turned[:1])], axis=0)
    return jnp.where(lane >= BLK - j, after, turned)


def halves(x):
    high = x.astype(BF16)
    return high, (x - high.astype(F32)).astype(BF16)


def dot(a, b, da, db):
    return lax.dot_general(a, b, (((da,), (db,)), ((), ())), preferred_element_type=F32)


def joined(states, table):
    sh, sl = halves(states)
    th, tl = halves(table)
    return dot(jnp.concatenate([sh, sh, sl], axis=0), jnp.concatenate([th, tl, th], axis=0), 0, 0)


ORDER = [(0, 0, 0), (1, 0, 0)]
for hop in range(1, ZN // 2):
    ORDER += [(0, 0, hop), (0, 1, hop), (1, 0, hop), (1, 1, hop)]
ORDER += [(0, 0, ZN // 2), (1, 1, ZN // 2)]
SLOT = {key: i for i, key in enumerate(ORDER)}
GROUP = 4
GROUPS = CHAN // GROUP


def mixer_kernel(
    q, k, v, sw, res, ld, w, g, gq_out, gkv_out, small_out,
    qkv, gbuf, swv, resv, ldv, slab, inb, wbuf, gst, xbuf, pout, pin, perm,
    xs, xr, gs, fs, gg, up, vp, cd, toep, gqs, gkvs, gqb, gkvb, smalls, smallb,
    local, qs, qr, gss, gsr, ws, wr, ls, lr, rs, rr, ps, pr, os, orr,
):
    p = lax.axis_index("pos")
    c = lax.axis_index("chan")
    h, x, core = p // ROW, (p // CORES) % XN, p % CORES
    l, z = c // ZN, c % ZN
    other = (1 - l) * ZN + z
    up_z, down_z = l * ZN + (z + 1) % ZN, l * ZN + (z + ZN - 1) % ZN
    sibling = p + 1 - 2 * core
    mine = x * CORES + core
    cols = w.shape[1]
    first_chan = p * OWN

    def wcols(slot):
        return wbuf.at[:, pl.ds(pl.multiple_of(slot * cols, cols), cols)]

    loads = [
        pltpu.make_async_copy(src, dst, local.at[i])
        for i, (src, dst) in enumerate(
            [(g, gbuf), (w, wcols(mine)), (q, qkv.at[0]), (k, qkv.at[1]), (v, qkv.at[2]),
             (sw, swv), (res, resv), (ld, ldv)]
        )
    ]
    for copy in loads:
        copy.start()

    barrier = pltpu.get_barrier_semaphore()

    @pl.loop(1, POS)
    def _(i):
        pl.semaphore_signal(barrier, 1, device_id={"pos": (p + i) % POS}, device_id_type=MESH)

    for d in (other, up_z, down_z):
        pl.semaphore_signal(barrier, 1, device_id={"chan": d}, device_id_type=MESH)

    loads[0].wait()
    wide = gbuf[...].astype(F32)
    part = wide.shape[1] // YH
    for i in range(YH):
        at = i * part
        gst[i] = jnp.concatenate(
            [wide[:, at : at + part // 2], wide[:, at + part // 2 : at + part]], axis=0
        ).astype(BF16)
    loads[1].wait()
    pl.semaphore_wait(barrier, POS - 1 + 3)

    first = []
    for i in range(1, YH):
        to = (h + i) % YH
        first.append(remote(gst.at[to], xbuf.at[0, h], gss.at[i - 1], gsr.at[i - 1],
                            pos=to * ROW + x * CORES + core))
        first[-1].start()
    weights = []
    for i in (1, 3, 2):
        to = h * ROW + ((x + i) % XN) * CORES + core
        weights.append(remote(wcols(mine), wcols(mine), ws.at[i - 1], wr.at[i - 1], pos=to))
        weights[-1].start()
    share = remote(wcols(mine), wcols(mine), ws.at[3], wr.at[3], pos=sibling)
    share.start()
    xbuf[0, h] = gst[h]

    for s in range(3):
        loads[2 + s].wait()
        slab[:, s] = qkv[s].astype(F32).T.astype(BF16).reshape(POS, OWN, BLK)

    for copy in first:
        copy.wait_recv()
    across = remote(xbuf.at[0], xbuf.at[1], ls, lr, chan=other)
    across.start()

    def ring(way, sel, hop):
        source = (sel, way if hop > 1 else 0, hop - 1)
        to = SLOT[(sel, way, hop)]
        return remote(xbuf.at[SLOT[source]], xbuf.at[to], rs.at[to], rr.at[to],
                      chan=up_z if way == 0 else down_z)

    hops = []

    def send(way, sel, hop):
        hops.append(ring(way, sel, hop))
        hops[-1].start()

    send(0, 0, 1)
    send(1, 0, 1)

    @pl.loop(1, POS)
    def _(i):
        to = (p + i) % POS
        remote(slab.at[to], inb.at[p], qs, qr, pos=to).start()

    inb[p] = slab[p]

    across.wait_recv()
    send(0, 1, 1)
    send(1, 1, 1)

    shared = []

    def share_weights(i):
        slot = ((x + XN - i) % XN) * CORES + core
        remote(wcols(slot), wcols(slot), ws.at[i - 1], wr.at[i - 1], pos=sibling).wait_recv()
        shared.append(remote(wcols(slot), wcols(slot), ws.at[3 + i], wr.at[3 + i], pos=sibling))
        shared[-1].start()

    def arrive(sel, hop):
        for way in (0, 1):
            if (sel, way, hop) in SLOT:
                ring(way, sel, hop).wait_recv()
                if (sel, way, hop + 1) in SLOT:
                    send(way, sel, hop + 1)

    half = xbuf.shape[3]
    rest_slots = pl.ds(0, POS - 1)

    def project(group):
        both = xbuf[pl.ds(group * GROUP, GROUP)].astype(F32).reshape(GROUP * YH, 2, 8, half)
        rows = jnp.concatenate(
            [both[:, 0].reshape(BLK, half), both[:, 1].reshape(BLK, half)], axis=1
        ).astype(BF16)
        pout[group] = dot(wbuf[...], rows, 1, 1).astype(BF16).reshape(POS, OWN, BLK)

        @pl.loop(1, POS)
        def _(i):
            to = (p + i) % POS
            remote(pout.at[group, to], pin.at[group, p], ps.at[group], pr.at[group], pos=to).start()

        pin[group, p] = pout[group, p]

    arrive(0, 1)
    share_weights(1)
    share_weights(3)
    arrive(1, 1)
    share_weights(2)
    arrive(0, 2)
    share.wait_recv()
    for copy in shared:
        copy.wait_recv()
    project(0)
    arrive(1, 2)
    project(1)

    for copy in loads[5:]:
        copy.wait()
    chans = swv.shape[2]
    pick = lax.broadcasted_iota(jnp.int32, (OWN, chans), 1) == (
        first_chan + lax.broadcasted_iota(jnp.int32, (OWN, chans), 0)
    )
    taps_of = [
        [
            jnp.sum(jnp.where(pick, swv[s, pl.ds(j, 1), :], 0.0), axis=1, keepdims=True)[None]
            for j in range(TAPS)
        ]
        for s in range(3)
    ]
    eye = (
        lax.broadcasted_iota(jnp.int32, (OWN, MODES, MODES), 1)
        == lax.broadcasted_iota(jnp.int32, (OWN, MODES, MODES), 2)
    )

    def columns(ref):
        own = pltpu.roll(ref[...], chans - first_chan, 1)[:, :BLK].T[:OWN]
        spread = jnp.where(eye, jnp.broadcast_to(own[:, None, :], eye.shape), 0.0)
        return jnp.sum(spread, axis=2, keepdims=True)

    shape3 = (OWN, MODES, BLK)
    time = lax.broadcasted_iota(jnp.int32, shape3, 2).astype(F32)
    weight = jnp.broadcast_to(columns(resv), shape3)
    rate = jnp.exp(jnp.broadcast_to(columns(ldv), shape3))
    near = jnp.exp(-rate * time)
    ahead = jnp.exp(-rate * (time + 1.0))
    back = jnp.exp(-rate * (BLK - 1.0 - time))
    taps = jnp.sum(weight * near, axis=1)
    t_ahead = (time + 1.0) * ahead
    t_back = (BLK - 1.0 - time) * back
    w_ahead = weight * ahead
    w_back = weight * back

    arrive(0, 3)
    remote(slab.at[rest_slots], inb.at[rest_slots], qs, qr, pos=sibling).wait()
    blocks = POS
    rows = blocks * OWN
    shape = (blocks, OWN, BLK)

    def stream(s):
        return inb[:, s].astype(F32)

    def conv(s):
        values = stream(s)
        return sum(taps_of[s][j] * later(values, j) for j in range(TAPS))

    xs[...] = (conv(1) * conv(2)).astype(BF16).astype(F32).reshape(rows, BLK)
    row2 = lax.broadcasted_iota(jnp.int32, (BLK, BLK), 0)
    lane2 = lax.broadcasted_iota(jnp.int32, (BLK, BLK), 1)
    flip = (row2 + lane2 == BLK - 1).astype(F32).astype(BF16)
    xr[...] = dot(xs[...].astype(BF16), flip, 1, 0)
    project(2)
    arrive(1, 3)

    fill = jnp.zeros((BLK - blocks, BLK), F32)

    def strided(i):
        return pl.ds(i, blocks, stride=OWN)

    for i in range(OWN):
        gated = xs[strided(i), :]
        turned = pltpu.roll(
            jnp.broadcast_to(taps[i : i + 1], (BLK, BLK)), 0, 1, stride=1, stride_axis=0
        )
        toep[i] = jnp.where(lane2 >= row2, turned, 0.0).astype(BF16)
        fs[pl.ds(i * blocks, blocks), :] = dot(gated.astype(BF16), toep[i], 1, 0)
        up[i] = dot(
            jnp.concatenate([*halves(back[i]), *halves(t_back[i])], axis=0),
            jnp.concatenate([gated, fill], axis=0).astype(BF16), 1, 1,
        )

    n = MODES
    s0, s1 = up[:, 0:n] + up[:, n : 2 * n], up[:, 2 * n : 3 * n] + up[:, 3 * n : 4 * n]
    falls = []
    for e in range(5):
        skip = 1 << e
        falls.append(jnp.exp(-rate * float(BLK * skip)))
        s0_k = pltpu.roll(s0, skip, 2)
        s1 = s1 + falls[e] * (pltpu.roll(s1, skip, 2) + float(BLK * skip) * s0_k)
        s0 = s0 + falls[e] * s0_k
    state, d_state = pltpu.roll(s0, 1, 2), pltpu.roll(s1, 1, 2)
    for i in range(OWN):
        xs[strided(i), :] = (
            fs[pl.ds(i * blocks, blocks), :] + joined(state[i], w_ahead[i])[:blocks]
        )

    lanes = GROUPS * BLK
    each = BLK // GROUP
    row_p = lax.broadcasted_iota(jnp.int32, (each, lanes), 0)
    lane_p = lax.broadcasted_iota(jnp.int32, (each, lanes), 1)
    for i, (sel, way, hop) in enumerate(ORDER):
        chip = (z + ZN - hop) % ZN if way == 0 else (z + hop) % ZN
        chunk = (l if sel == 0 else 1 - l) * ZN + chip
        goes = (row_p // 8) * BLK + chunk * 8 + row_p % 8
        perm[pl.ds(i * each, each), :] = (lane_p == goes).astype(F32).astype(BF16)

    for sel, way, hop in ORDER[-2:]:
        ring(way, sel, hop).wait_recv()
    project(3)

    own_rows = ROW * OWN
    tiles = []
    for i in range(GROUPS):
        remote(pout.at[i, rest_slots], pin.at[i, rest_slots], ps.at[i], pr.at[i], pos=sibling).wait()
        total = sum(pin[i, pl.ds(j * ROW, ROW)].astype(F32) for j in range(YH))
        tiles.append(total.reshape(own_rows, BLK).astype(BF16))
    ordered = dot(jnp.concatenate(tiles, axis=1), perm[...], 1, 0)
    mix = jnp.concatenate(
        [ordered[:, i * BLK : (i + 1) * BLK].reshape(ROW, OWN, BLK) for i in range(YH)], axis=0
    )

    lane = lax.broadcasted_iota(jnp.int32, (OWN, BLK), 1)
    sums = []

    def finish_stream(s, grad, ref, index):
        values = stream(s)
        total = sum(taps_of[s][j] * sooner(grad, j) for j in range(TAPS)).astype(BF16)
        if index is None:
            ref[...] = total
        else:
            ref[:, index] = total
        for j in range(TAPS):
            sums.append(
                jnp.sum(jnp.sum(grad * later(values, j), axis=0), axis=1, keepdims=True)
            )

    def give(mine_ref, all_ref, sem):
        @pl.loop(1, POS)
        def _(i):
            to = (p + i) % POS
            remote(mine_ref.at[to], all_ref.at[p], os.at[sem], orr.at[sem], pos=to).start()

        all_ref[p] = mine_ref[p]

    finish_stream(0, mix * xs[...].reshape(shape), gqs, None)
    give(gqs, gqb, 0)

    gs[...] = (mix * conv(0).astype(BF16).astype(F32)).astype(BF16).astype(F32).reshape(rows, BLK)
    for i in range(OWN):
        grad = gs[strided(i), :]
        low = grad.astype(BF16)
        gg[pl.ds(i * blocks, blocks), :] = dot(low, toep[i], 1, 1)
        vp[i] = dot(
            jnp.concatenate([*halves(ahead[i]), *halves(t_ahead[i])], axis=0),
            jnp.concatenate([grad, fill], axis=0).astype(BF16), 1, 1,
        )
    t0, t1 = vp[:, 0:n] + vp[:, n : 2 * n], vp[:, 2 * n : 3 * n] + vp[:, 3 * n : 4 * n]
    rest = t0
    for e in range(5):
        rest = rest + falls[e] * pltpu.roll(rest, BLK - (1 << e), 2)
    rest = pltpu.roll(rest, BLK - 1, 2)
    for i in range(OWN):
        pair = dot(xr[strided(i), :].astype(BF16), gs[strided(i), :].astype(BF16), 0, 0)
        turned = pltpu.roll(pair, 1, 1, stride=1, stride_axis=0)
        cd[pl.ds(i, 1), :] = jnp.sum(jnp.where(lane2 <= row2, turned, 0.0), axis=0, keepdims=True)
        xs[strided(i), :] = (
            gg[pl.ds(i * blocks, blocks), :] + joined(rest[i], w_back[i])[:blocks]
        )
    grad_gated = xs[...].reshape(shape)
    finish_stream(1, grad_gated * conv(2), gkvs, 0)
    finish_stream(2, grad_gated * conv(1), gkvs, 1)
    give(gkvs, gkvb, 1)

    corr = cd[...][:, None, :] * near
    by_res = jnp.sum(corr + t0 * state, axis=2, keepdims=True)
    by_rate = jnp.sum(corr * time + t1 * state + t0 * d_state, axis=2, keepdims=True)
    by_log = -by_rate * weight * rate
    lane3 = lax.broadcasted_iota(jnp.int32, shape3, 2)
    mode3 = lax.broadcasted_iota(jnp.int32, shape3, 1)
    tiny = jnp.sum(
        jnp.where(lane3 == 16 + mode3, by_res, jnp.where(lane3 == 32 + mode3, by_log, 0.0)), axis=1
    )
    for j, total in enumerate(sums):
        tiny = jnp.where(lane == j, total, tiny)
    smalls[...] = jnp.where(lane[:8] < BLK // 2, tiny[:8], pltpu.roll(tiny[8:], BLK // 2, 1))

    @pl.loop(1, POS)
    def _(i):
        to = (p + i) % POS
        remote(smalls, smallb.at[p], os.at[2], orr.at[2], pos=to).start()

    smallb[p] = smalls[...]

    for copy in first + weights + [share, across] + hops + shared:
        copy.wait_send()
    for sem, (ref, out) in enumerate(((gqb, gq_out), (gkvb, gkv_out), (smallb, small_out))):
        remote(ref.at[rest_slots], ref.at[rest_slots], os.at[sem], orr.at[sem], pos=sibling).wait()
        out[...] = ref[...]


def mixer(q, k, v, short_weights, residues, log_decay, w, g):
    chans, cols = w.shape
    dma = pltpu.SemaphoreType.DMA
    half = g.shape[1] // YH // 2
    rows = POS * OWN
    outs = [((POS, OWN, BLK), BF16), ((POS, 2, OWN, BLK), BF16), ((POS, 8, BLK), F32)]
    return pl.pallas_call(
        mixer_kernel,
        out_shape=tuple(jax.ShapeDtypeStruct(*o) for o in outs),
        in_specs=[full(pl.ANY)] * 8,
        out_specs=(full(),) * 3,
        scratch_shapes=[
            pltpu.VMEM((3, BLK, chans), BF16),
            pltpu.VMEM(g.shape, BF16),
            pltpu.VMEM(short_weights.shape, F32),
            pltpu.VMEM(residues.shape, F32),
            pltpu.VMEM(log_decay.shape, F32),
            pltpu.VMEM((POS, 3, OWN, BLK), BF16),
            pltpu.VMEM((POS, 3, OWN, BLK), BF16),
            pltpu.VMEM((chans, ROW * cols), BF16),
            pltpu.VMEM((YH, 16, half), BF16),
            pltpu.VMEM((CHAN, YH, 16, half), BF16),
            pltpu.VMEM((GROUPS, POS, OWN, BLK), BF16),
            pltpu.VMEM((GROUPS, POS, OWN, BLK), BF16),
            pltpu.VMEM((GROUPS * BLK, GROUPS * BLK), BF16),
        ]
        + [pltpu.VMEM((rows, BLK), F32)] * 5
        + [pltpu.VMEM((OWN, 4 * MODES, BLK), F32)] * 2
        + [pltpu.VMEM((OWN, BLK), F32), pltpu.VMEM((OWN, BLK, BLK), BF16)]
        + [pltpu.VMEM(*o) for o in (outs[0], outs[1], outs[0], outs[1])]
        + [pltpu.VMEM((8, BLK), F32), pltpu.VMEM(*outs[2])]
        + [
            dma((8,)),
            dma, dma,
            dma((YH - 1,)), dma((YH - 1,)),
            dma((7,)), dma((7,)),
            dma, dma,
            dma((CHAN,)), dma((CHAN,)),
            dma((GROUPS,)), dma((GROUPS,)),
            dma((3,)), dma((3,)),
        ],
        compiler_params=pltpu.CompilerParams(
            collective_id=0, has_side_effects=True, vmem_limit_bytes=48 * 1024 * 1024
        ),
        name="mixer",
    )(q, k, v, short_weights, residues, log_decay, w, g)


def finish_kernel(gq, gkv, small, q, k, v, short, res, dec):
    chans = POS * OWN
    q[...] = gq[...].astype(F32).reshape(chans, BLK).T.astype(BF16)
    for s, ref in enumerate((k, v)):
        ref[...] = gkv[:, s].astype(F32).reshape(chans, BLK).T.astype(BF16)
    packed = small[...]
    both = jnp.concatenate([packed, pltpu.roll(packed, BLK // 2, 2)], axis=1)
    turned = both.reshape(chans, BLK).T
    res[...] = turned[16:32]
    dec[...] = turned[32:48]
    for s in range(3):
        short[s] = turned[s * TAPS : (s + 1) * TAPS]


def finish(gq, gkv, small):
    chans = POS * OWN
    stream = jax.ShapeDtypeStruct((BLK, chans), BF16)
    mode = jax.ShapeDtypeStruct((MODES, chans), F32)
    return pl.pallas_call(
        finish_kernel,
        out_shape=(stream, stream, stream, jax.ShapeDtypeStruct((3, TAPS, chans), F32), mode, mode),
        in_specs=[full()] * 3,
        out_specs=(full(),) * 6,
        compiler_params=pltpu.CompilerParams(vmem_limit_bytes=48 * 1024 * 1024),
        name="finish",
    )(gq, gkv, small)


def local(q_in, k_in, v_in, short_weights, residues, log_decay, out_weight, grad_out):
    parts = mixer(
        q_in, k_in, v_in, short_weights, residues.T, log_decay.T, out_weight, grad_out
    )
    gq, gk, gv, short, res, dec = finish(*parts)
    return gq, gk, gv, short, res.T, dec.T


def solution(mesh):
    in_specs = (
        P("pos", "chan"),
        P("pos", "chan"),
        P("pos", "chan"),
        P(None, None, "chan"),
        P("chan", None),
        P("chan", None),
        P("chan", "pos"),
        P(("pos", "chan"), None),
    )
    out_specs = (
        P("pos", "chan"),
        P("pos", "chan"),
        P("pos", "chan"),
        P(None, None, "chan"),
        P("chan", None),
        P("chan", None),
    )
    return jax.shard_map(local, mesh=mesh, in_specs=in_specs, out_specs=out_specs, check_vma=False)
```

```python
import functools

import jax
import jax.numpy as jnp
from jax import lax
from jax.experimental import pallas as pl
from jax.experimental.pallas import tpu as pltpu
from jax.sharding import PartitionSpec as P

F32 = jnp.float32
BF16 = jnp.bfloat16
MESH = pl.DeviceIdType.MESH

YH, XN, CORES = 4, 4, 2
YL, ZN = 2, 8
POS = YH * XN * CORES
CHAN = YL * ZN
ROW = XN * CORES
BLK = 128
OWN = 16
MODES = 16
TAPS = 3
VMEM = 60 * 1024 * 1024


def remote(src, dst, send, recv, **device):
    return pltpu.make_async_remote_copy(
        src_ref=src, dst_ref=dst, send_sem=send, recv_sem=recv,
        device_id=device, device_id_type=MESH,
    )


def full(memory=pltpu.VMEM):
    return pl.BlockSpec(memory_space=memory)


def later(x, j):
    if j == 0:
        return x
    lane = lax.broadcasted_iota(jnp.int32, x.shape, 2)
    turned = pltpu.roll(x, j, 2)
    before = jnp.concatenate([jnp.zeros_like(turned[:1]), turned[:-1]], axis=0)
    return jnp.where(lane < j, before, turned)


def sooner(x, j):
    if j == 0:
        return x
    lane = lax.broadcasted_iota(jnp.int32, x.shape, 2)
    turned = pltpu.roll(x, BLK - j, 2)
    after = jnp.concatenate([turned[1:], jnp.zeros_like(turned[:1])], axis=0)
    return jnp.where(lane >= BLK - j, after, turned)


def halves(x):
    high = x.astype(BF16)
    return high, (x - high.astype(F32)).astype(BF16)


def dot(a, b, da, db):
    return lax.dot_general(a, b, (((da,), (db,)), ((), ())), preferred_element_type=F32)


def joined(states, table):
    sh, sl = halves(states)
    th, tl = halves(table)
    return dot(jnp.concatenate([sh, sh, sl], axis=0), jnp.concatenate([th, tl, th], axis=0), 0, 0)


ORDER = [(0, 0, 0), (1, 0, 0)]
for hop in range(1, ZN // 2):
    ORDER += [(0, 0, hop), (0, 1, hop), (1, 0, hop), (1, 1, hop)]
ORDER += [(0, 0, ZN // 2), (1, 1, ZN // 2)]
SLOT = {key: i for i, key in enumerate(ORDER)}
NEAR = (0, 1, 3, 2)
GROUP = 4
GROUPS = CHAN // GROUP
PARTS = ((0, 2), (2, 1), (3, 1))


def mixer_kernel(
    q, k, v, sw, res, ld, w, g, gq_out, gkv_out, small_out,
    qkv, gbuf, swv, resv, ldv, slab, inb, wbuf, gst, xbuf, pout, pin, perm,
    xs, xr, gs, fs, gg, up, vp, cd, toep, gqs, gkvs, gqb, gkvb, smalls, smallb,
    local, qs, qr, gss, gsr, ws, wr, ls, lr, rs, rr, ps, pr, os, orr,
):
    p = lax.axis_index("pos")
    c = lax.axis_index("chan")
    h, x, core = p // ROW, (p // CORES) % XN, p % CORES
    l, z = c // ZN, c % ZN
    other = (1 - l) * ZN + z
    up_z, down_z = l * ZN + (z + 1) % ZN, l * ZN + (z + ZN - 1) % ZN
    sibling = p + 1 - 2 * core
    mine = x * CORES + core
    cols = w.shape[1]
    first_chan = p * OWN

    def wcols(slot):
        return wbuf.at[:, pl.ds(pl.multiple_of(slot * cols, cols), cols)]

    loads = [
        pltpu.make_async_copy(src, dst, local.at[i])
        for i, (src, dst) in enumerate(
            [(g, gbuf), (w, wcols(mine)), (q, qkv.at[0]), (k, qkv.at[1]), (v, qkv.at[2]),
             (sw, swv), (res, resv), (ld, ldv)]
        )
    ]
    for copy in loads:
        copy.start()

    barrier = pltpu.get_barrier_semaphore()

    @pl.loop(1, POS)
    def _(i):
        pl.semaphore_signal(barrier, 1, device_id={"pos": (p + i) % POS}, device_id_type=MESH)

    for d in (other, up_z, down_z):
        pl.semaphore_signal(barrier, 1, device_id={"chan": d}, device_id_type=MESH)

    loads[0].wait()
    wide = gbuf[...].astype(F32)
    part = wide.shape[1] // YH
    for i in range(YH):
        at = i * part
        gst[i] = jnp.concatenate(
            [wide[:, at : at + part // 2], wide[:, at + part // 2 : at + part]], axis=0
        ).astype(BF16)
    loads[1].wait()
    pl.semaphore_wait(barrier, POS - 1 + 3)

    xbuf[0, h] = gst[h]

    def piece(r):
        return (h + YH - NEAR[r]) % YH

    def ring(way, sel, hop, r):
        source = (sel, way if hop > 1 else 0, hop - 1)
        to = SLOT[(sel, way, hop)]
        return remote(xbuf.at[SLOT[source], piece(r)], xbuf.at[to, piece(r)],
                      rs.at[to * YH + r], rr.at[to * YH + r],
                      chan=up_z if way == 0 else down_z)

    hops, across = [], []

    def send(way, sel, hop, r):
        hops.append(ring(way, sel, hop, r))
        hops[-1].start()

    def pass_own(r):
        send(0, 0, 1, r)
        send(1, 0, 1, r)
        across.append(remote(xbuf.at[0, piece(r)], xbuf.at[1, piece(r)], ls.at[r], lr.at[r],
                             chan=other))
        across[-1].start()

    first = []
    for i in range(1, YH):
        to = (h + NEAR[i]) % YH
        first.append(remote(gst.at[to], xbuf.at[0, h], gss.at[i - 1], gsr.at[i - 1],
                            pos=to * ROW + x * CORES + core))
        first[-1].start()
    pass_own(0)
    weights = []
    for i in (1, 3, 2):
        to = h * ROW + ((x + i) % XN) * CORES + core
        weights.append(remote(wcols(mine), wcols(mine), ws.at[i - 1], wr.at[i - 1], pos=to))
        weights[-1].start()
    share = remote(wcols(mine), wcols(mine), ws.at[3], wr.at[3], pos=sibling)
    share.start()

    for s in range(3):
        loads[2 + s].wait()
        slab[:, s] = qkv[s].astype(F32).T.astype(BF16).reshape(POS, OWN, BLK)
        first[s].wait_recv()
        pass_own(s + 1)

    @pl.loop(1, POS)
    def _(i):
        to = (p + i) % POS
        remote(slab.at[to], inb.at[p], qs, qr, pos=to).start()

    inb[p] = slab[p]

    shared = []

    def share_weights(i):
        slot = ((x + XN - i) % XN) * CORES + core
        remote(wcols(slot), wcols(slot), ws.at[i - 1], wr.at[i - 1], pos=sibling).wait_recv()
        shared.append(remote(wcols(slot), wcols(slot), ws.at[3 + i], wr.at[3 + i], pos=sibling))
        shared[-1].start()

    def arrive(sel, hop, *work):
        for r in range(YH):
            for way in (0, 1):
                if (sel, way, hop) in SLOT:
                    ring(way, sel, hop, r).wait_recv()
                    if (sel, way, hop + 1) in SLOT:
                        send(way, sel, hop + 1, r)
            if r < len(work):
                work[r]()

    half = xbuf.shape[3]
    rest_slots = pl.ds(0, POS - 1)

    def product(tile):
        both = xbuf[pl.ds(tile * GROUP, GROUP)].astype(F32).reshape(GROUP * YH, 2, 8, half)
        rows = jnp.concatenate(
            [both[:, 0].reshape(BLK, half), both[:, 1].reshape(BLK, half)], axis=1
        ).astype(BF16)
        pout[:, tile] = dot(wbuf[...], rows, 1, 1).astype(BF16).reshape(POS, OWN, BLK)

    def give_part(part):
        tiles = pl.ds(*PARTS[part])

        @pl.loop(1, POS)
        def _(i):
            to = (p + i) % POS
            remote(pout.at[to, tiles], pin.at[p, tiles], ps.at[part], pr.at[part], pos=to).start()

        pin[p, tiles] = pout[p, tiles]

    for r in range(YH):
        across[r].wait_recv()
        send(0, 1, 1, r)
        send(1, 1, 1, r)

    for copy in loads[5:]:
        copy.wait()
    chans = swv.shape[2]
    pick = lax.broadcasted_iota(jnp.int32, (OWN, chans), 1) == (
        first_chan + lax.broadcasted_iota(jnp.int32, (OWN, chans), 0)
    )
    taps_of = [
        [
            jnp.sum(jnp.where(pick, swv[s, pl.ds(j, 1), :], 0.0), axis=1, keepdims=True)[None]
            for j in range(TAPS)
        ]
        for s in range(3)
    ]
    eye = (
        lax.broadcasted_iota(jnp.int32, (OWN, MODES, MODES), 1)
        == lax.broadcasted_iota(jnp.int32, (OWN, MODES, MODES), 2)
    )

    def columns(ref):
        own = pltpu.roll(ref[...], chans - first_chan, 1)[:, :BLK].T[:OWN]
        spread = jnp.where(eye, jnp.broadcast_to(own[:, None, :], eye.shape), 0.0)
        return jnp.sum(spread, axis=2, keepdims=True)

    shape3 = (OWN, MODES, BLK)
    time = lax.broadcasted_iota(jnp.int32, shape3, 2).astype(F32)
    weight = jnp.broadcast_to(columns(resv), shape3)
    rate = jnp.exp(jnp.broadcast_to(columns(ldv), shape3))
    near = jnp.exp(-rate * time)
    ahead = jnp.exp(-rate * (time + 1.0))
    back = jnp.exp(-rate * (BLK - 1.0 - time))
    taps = jnp.sum(weight * near, axis=1)
    t_ahead = (time + 1.0) * ahead
    t_back = (BLK - 1.0 - time) * back
    w_ahead = weight * ahead
    w_back = weight * back

    arrive(0, 1)
    arrive(1, 1)
    remote(slab.at[rest_slots], inb.at[rest_slots], qs, qr, pos=sibling).wait()
    blocks = POS
    rows = blocks * OWN
    shape = (blocks, OWN, BLK)
    row2 = lax.broadcasted_iota(jnp.int32, (BLK, BLK), 0)
    lane2 = lax.broadcasted_iota(jnp.int32, (BLK, BLK), 1)
    fill = jnp.zeros((BLK - blocks, BLK), F32)
    held = {}

    def stream(s):
        return inb[:, s].astype(F32)

    def conv(s):
        values = stream(s)
        return sum(taps_of[s][j] * later(values, j) for j in range(TAPS))

    def strided(i):
        return pl.ds(i, blocks, stride=OWN)

    def gate():
        xs[...] = (conv(1) * conv(2)).astype(BF16).astype(F32).reshape(rows, BLK)

    def within(low, high):
        def work():
            for i in range(low, high):
                gated = xs[strided(i), :]
                turned = pltpu.roll(
                    jnp.broadcast_to(taps[i : i + 1], (BLK, BLK)), 0, 1, stride=1, stride_axis=0
                )
                toep[i] = jnp.where(lane2 >= row2, turned, 0.0).astype(BF16)
                fs[pl.ds(i * blocks, blocks), :] = dot(gated.astype(BF16), toep[i], 1, 0)
                up[i] = dot(
                    jnp.concatenate([*halves(back[i]), *halves(t_back[i])], axis=0),
                    jnp.concatenate([gated, fill], axis=0).astype(BF16), 1, 1,
                )
        return work

    n = MODES

    def edges():
        flip = (row2 + lane2 == BLK - 1).astype(F32).astype(BF16)
        xr[...] = dot(xs[...].astype(BF16), flip, 1, 0)
        s0 = up[:, 0:n] + up[:, n : 2 * n]
        s1 = up[:, 2 * n : 3 * n] + up[:, 3 * n : 4 * n]
        held["falls"] = falls = []
        for e in range(5):
            skip = 1 << e
            falls.append(jnp.exp(-rate * float(BLK * skip)))
            s0_k = pltpu.roll(s0, skip, 2)
            s1 = s1 + falls[e] * (pltpu.roll(s1, skip, 2) + float(BLK * skip) * s0_k)
            s0 = s0 + falls[e] * s0_k
        held["state"], held["d_state"] = pltpu.roll(s0, 1, 2), pltpu.roll(s1, 1, 2)

    def between(low, high):
        def work():
            for i in range(low, high):
                xs[strided(i), :] = (
                    fs[pl.ds(i * blocks, blocks), :]
                    + joined(held["state"][i], w_ahead[i])[:blocks]
                )
        return work

    lanes = GROUPS * BLK
    each = BLK // GROUP

    def order():
        row_p = lax.broadcasted_iota(jnp.int32, (each, lanes), 0)
        lane_p = lax.broadcasted_iota(jnp.int32, (each, lanes), 1)
        for i, (sel, way, hop) in enumerate(ORDER):
            chip = (z + ZN - hop) % ZN if way == 0 else (z + hop) % ZN
            chunk = (l if sel == 0 else 1 - l) * ZN + chip
            goes = (row_p // 8) * BLK + chunk * 8 + row_p % 8
            perm[pl.ds(i * each, each), :] = (lane_p == goes).astype(F32).astype(BF16)

    def weights_in():
        share.wait_recv()
        for copy in shared:
            copy.wait_recv()
        product(0)

    half_own = OWN // 2
    for i in (1, 3, 2):
        share_weights(i)
    arrive(0, 2, gate, within(0, 5), within(5, 11), within(11, OWN))
    arrive(1, 2, weights_in, lambda: product(1), lambda: give_part(0), edges)
    arrive(0, 3, between(0, half_own), between(half_own, OWN), order)
    arrive(1, 3, lambda: product(2), lambda: give_part(1))
    for r in range(YH):
        for sel, way, hop in ORDER[-2:]:
            ring(way, sel, hop, r).wait_recv()
    product(3)
    give_part(2)
    falls, state, d_state = held["falls"], held["state"], held["d_state"]

    own_rows = ROW * OWN
    tiles = []
    for part, (first_tile, count) in enumerate(PARTS):
        some = (rest_slots, pl.ds(first_tile, count))
        remote(pout.at[some], pin.at[some], ps.at[part], pr.at[part], pos=sibling).wait()
        for i in range(first_tile, first_tile + count):
            total = sum(pin[pl.ds(j * ROW, ROW), i].astype(F32) for j in range(YH))
            tiles.append(total.reshape(own_rows, BLK).astype(BF16))
    ordered = dot(jnp.concatenate(tiles, axis=1), perm[...], 1, 0)
    mix = jnp.concatenate(
        [ordered[:, i * BLK : (i + 1) * BLK].reshape(ROW, OWN, BLK) for i in range(YH)], axis=0
    )

    lane = lax.broadcasted_iota(jnp.int32, (OWN, BLK), 1)
    sums = []

    def finish_stream(s, grad, ref, index):
        values = stream(s)
        total = sum(taps_of[s][j] * sooner(grad, j) for j in range(TAPS)).astype(BF16)
        if index is None:
            ref[...] = total
        else:
            ref[:, index] = total
        for j in range(TAPS):
            sums.append(jnp.sum(grad * later(values, j), axis=0))

    def give(mine_ref, all_ref, sem):
        @pl.loop(1, POS)
        def _(i):
            to = (p + i) % POS
            remote(mine_ref.at[to], all_ref.at[p], os.at[sem], orr.at[sem], pos=to).start()

        all_ref[p] = mine_ref[p]

    finish_stream(0, mix * xs[...].reshape(shape), gqs, None)
    give(gqs, gqb, 0)

    gs[...] = (mix * conv(0).astype(BF16).astype(F32)).astype(BF16).astype(F32).reshape(rows, BLK)
    for i in range(OWN):
        grad = gs[strided(i), :]
        low = grad.astype(BF16)
        gg[pl.ds(i * blocks, blocks), :] = dot(low, toep[i], 1, 1)
        vp[i] = dot(
            jnp.concatenate([*halves(ahead[i]), *halves(t_ahead[i])], axis=0),
            jnp.concatenate([grad, fill], axis=0).astype(BF16), 1, 1,
        )
    t0, t1 = vp[:, 0:n] + vp[:, n : 2 * n], vp[:, 2 * n : 3 * n] + vp[:, 3 * n : 4 * n]
    rest = t0
    for e in range(5):
        rest = rest + falls[e] * pltpu.roll(rest, BLK - (1 << e), 2)
    rest = pltpu.roll(rest, BLK - 1, 2)
    for i in range(OWN):
        xs[strided(i), :] = (
            gg[pl.ds(i * blocks, blocks), :] + joined(rest[i], w_back[i])[:blocks]
        )
    grad_gated = xs[...].reshape(shape)
    finish_stream(1, grad_gated * conv(2), gkvs, 0)
    finish_stream(2, grad_gated * conv(1), gkvs, 1)
    give(gkvs, gkvb, 1)

    for i in range(OWN):
        pair = dot(xr[strided(i), :].astype(BF16), gs[strided(i), :].astype(BF16), 0, 0)
        turned = pltpu.roll(pair, 1, 1, stride=1, stride_axis=0)
        cd[pl.ds(i, 1), :] = jnp.sum(jnp.where(lane2 <= row2, turned, 0.0), axis=0, keepdims=True)
    corr = cd[...][:, None, :] * near
    by_res = jnp.sum(corr + t0 * state, axis=2, keepdims=True)
    by_rate = jnp.sum(corr * time + t1 * state + t0 * d_state, axis=2, keepdims=True)
    by_log = -by_rate * weight * rate
    lane3 = lax.broadcasted_iota(jnp.int32, shape3, 2)
    mode3 = lax.broadcasted_iota(jnp.int32, shape3, 1)
    tiny = jnp.sum(
        jnp.where(lane3 == 16 + mode3, by_res, jnp.where(lane3 == 32 + mode3, by_log, 0.0)), axis=1
    )
    for j, total in enumerate(sums):
        tiny = jnp.where(lane == j, jnp.sum(total, axis=1, keepdims=True), tiny)
    smalls[...] = jnp.where(lane[:8] < BLK // 2, tiny[:8], pltpu.roll(tiny[8:], BLK // 2, 1))

    @pl.loop(1, POS)
    def _(i):
        to = (p + i) % POS
        remote(smalls, smallb.at[p], os.at[2], orr.at[2], pos=to).start()

    smallb[p] = smalls[...]

    for copy in first + weights + [share] + across + hops + shared:
        copy.wait_send()
    for sem, (ref, out) in enumerate(((gqb, gq_out), (gkvb, gkv_out), (smallb, small_out))):
        remote(ref.at[rest_slots], ref.at[rest_slots], os.at[sem], orr.at[sem], pos=sibling).wait()
        out[...] = ref[...]


def mixer(q, k, v, short_weights, residues, log_decay, w, g):
    chans, cols = w.shape
    dma = pltpu.SemaphoreType.DMA
    half = g.shape[1] // YH // 2
    rows = POS * OWN
    outs = [((POS, OWN, BLK), BF16), ((POS, 2, OWN, BLK), BF16), ((POS, 8, BLK), F32)]
    return pl.pallas_call(
        mixer_kernel,
        out_shape=tuple(jax.ShapeDtypeStruct(*o) for o in outs),
        in_specs=[full(pl.ANY)] * 8,
        out_specs=(full(),) * 3,
        scratch_shapes=[
            pltpu.VMEM((3, BLK, chans), BF16),
            pltpu.VMEM(g.shape, BF16),
            pltpu.VMEM(short_weights.shape, F32),
            pltpu.VMEM(residues.shape, F32),
            pltpu.VMEM(log_decay.shape, F32),
            pltpu.VMEM((POS, 3, OWN, BLK), BF16),
            pltpu.VMEM((POS, 3, OWN, BLK), BF16),
            pltpu.VMEM((chans, ROW * cols), BF16),
            pltpu.VMEM((YH, 16, half), BF16),
            pltpu.VMEM((CHAN, YH, 16, half), BF16),
            pltpu.VMEM((POS, GROUPS, OWN, BLK), BF16),
            pltpu.VMEM((POS, GROUPS, OWN, BLK), BF16),
            pltpu.VMEM((GROUPS * BLK, GROUPS * BLK), BF16),
        ]
        + [pltpu.VMEM((rows, BLK), F32)] * 5
        + [pltpu.VMEM((OWN, 4 * MODES, BLK), F32)] * 2
        + [pltpu.VMEM((OWN, BLK), F32), pltpu.VMEM((OWN, BLK, BLK), BF16)]
        + [pltpu.VMEM(*o) for o in (outs[0], outs[1], outs[0], outs[1])]
        + [pltpu.VMEM((8, BLK), F32), pltpu.VMEM(*outs[2])]
        + [
            dma((8,)),
            dma, dma,
            dma((YH - 1,)), dma((YH - 1,)),
            dma((7,)), dma((7,)),
            dma((YH,)), dma((YH,)),
            dma((CHAN * YH,)), dma((CHAN * YH,)),
            dma((len(PARTS),)), dma((len(PARTS),)),
            dma((3,)), dma((3,)),
        ],
        compiler_params=pltpu.CompilerParams(
            collective_id=0, has_side_effects=True, vmem_limit_bytes=VMEM
        ),
        name="mixer",
    )(q, k, v, short_weights, residues, log_decay, w, g)


def finish_kernel(gq_in, gkv_in, small_in, q, k, v, short, res, dec, gq, gkv, small, local):
    chans = POS * OWN
    loads = [
        pltpu.make_async_copy(src, dst, local.at[i])
        for i, (src, dst) in enumerate([(gq_in, gq), (gkv_in, gkv), (small_in, small)])
    ]
    for copy in loads:
        copy.start()
    loads[0].wait()
    q[...] = gq[...].astype(F32).reshape(chans, BLK).T.astype(BF16)
    loads[1].wait()
    for s, ref in enumerate((k, v)):
        ref[...] = gkv[:, s].astype(F32).reshape(chans, BLK).T.astype(BF16)
    loads[2].wait()
    packed = small[...]
    both = jnp.concatenate([packed, pltpu.roll(packed, BLK // 2, 2)], axis=1)
    turned = both.reshape(chans, BLK).T
    res[...] = turned[16:32]
    dec[...] = turned[32:48]
    for s in range(3):
        short[s] = turned[s * TAPS : (s + 1) * TAPS]


def finish(gq, gkv, small):
    chans = POS * OWN
    stream = jax.ShapeDtypeStruct((BLK, chans), BF16)
    mode = jax.ShapeDtypeStruct((MODES, chans), F32)
    return pl.pallas_call(
        finish_kernel,
        out_shape=(stream, stream, stream, jax.ShapeDtypeStruct((3, TAPS, chans), F32), mode, mode),
        in_specs=[full(pl.ANY)] * 3,
        out_specs=(full(),) * 6,
        scratch_shapes=[pltpu.VMEM(a.shape, a.dtype) for a in (gq, gkv, small)]
        + [pltpu.SemaphoreType.DMA((3,))],
        compiler_params=pltpu.CompilerParams(vmem_limit_bytes=VMEM),
        name="finish",
    )(gq, gkv, small)


def local(q_in, k_in, v_in, short_weights, residues, log_decay, out_weight, grad_out):
    parts = mixer(
        q_in, k_in, v_in, short_weights, residues.T, log_decay.T, out_weight, grad_out
    )
    gq, gk, gv, short, res, dec = finish(*parts)
    return gq, gk, gv, short, res.T, dec.T


def solution(mesh):
    in_specs = (
        P("pos", "chan"),
        P("pos", "chan"),
        P("pos", "chan"),
        P(None, None, "chan"),
        P("chan", None),
        P("chan", None),
        P("chan", "pos"),
        P(("pos", "chan"), None),
    )
    out_specs = (
        P("pos", "chan"),
        P("pos", "chan"),
        P("pos", "chan"),
        P(None, None, "chan"),
        P("chan", None),
        P("chan", None),
    )
    return jax.shard_map(local, mesh=mesh, in_specs=in_specs, out_specs=out_specs, check_vma=False)
```

```python
import functools

import jax
import jax.numpy as jnp
from jax import lax
from jax.experimental import pallas as pl
from jax.experimental.pallas import tpu as pltpu
from jax.sharding import PartitionSpec as P

F32 = jnp.float32
BF16 = jnp.bfloat16
MESH = pl.DeviceIdType.MESH

YH, XN, CORES = 4, 4, 2
YL, ZN = 2, 8
POS = YH * XN * CORES
CHAN = YL * ZN
ROW = XN * CORES
BLK = 128
OWN = 16
MODES = 16
TAPS = 3
VMEM = 60 * 1024 * 1024


def remote(src, dst, send, recv, **device):
    return pltpu.make_async_remote_copy(
        src_ref=src, dst_ref=dst, send_sem=send, recv_sem=recv,
        device_id=device, device_id_type=MESH,
    )


def full(memory=pltpu.VMEM):
    return pl.BlockSpec(memory_space=memory)


def later(x, j):
    if j == 0:
        return x
    lane = lax.broadcasted_iota(jnp.int32, x.shape, 2)
    turned = pltpu.roll(x, j, 2)
    before = jnp.concatenate([jnp.zeros_like(turned[:1]), turned[:-1]], axis=0)
    return jnp.where(lane < j, before, turned)


def sooner(x, j):
    if j == 0:
        return x
    lane = lax.broadcasted_iota(jnp.int32, x.shape, 2)
    turned = pltpu.roll(x, BLK - j, 2)
    after = jnp.concatenate([turned[1:], jnp.zeros_like(turned[:1])], axis=0)
    return jnp.where(lane >= BLK - j, after, turned)


def halves(x):
    high = x.astype(BF16)
    return high, (x - high.astype(F32)).astype(BF16)


def dot(a, b, da, db):
    return lax.dot_general(a, b, (((da,), (db,)), ((), ())), preferred_element_type=F32)


def joined(states, table):
    sh, sl = halves(states)
    th, tl = halves(table)
    return dot(jnp.concatenate([sh, sh, sl], axis=0), jnp.concatenate([th, tl, th], axis=0), 0, 0)


ORDER = [(0, 0, 0), (1, 0, 0)]
for hop in range(1, ZN // 2):
    ORDER += [(0, 0, hop), (0, 1, hop), (1, 0, hop), (1, 1, hop)]
ORDER += [(0, 0, ZN // 2), (1, 1, ZN // 2)]
SLOT = {key: i for i, key in enumerate(ORDER)}
NEAR = (0, 1, 3, 2)
GROUP = 4
GROUPS = CHAN // GROUP
PARTS = ((0, 2), (2, 1), (3, 1))


def mixer_kernel(
    q, k, v, sw, res, ld, w, g, gq_out, gkv_out, small_out,
    qkv, gbuf, swv, resv, ldv, slab, inb, wbuf, gst, xbuf, pout, pin, perm,
    xs, xr, gs, fs, gg, up, vp, cd, toep, gqs, gkvs, gqb, gkvb, smalls, smallb,
    local, qs, qr, gss, gsr, ws, wr, ls, lr, rs, rr, ps, pr, os, orr,
):
    p = lax.axis_index("pos")
    c = lax.axis_index("chan")
    h, x, core = p // ROW, (p // CORES) % XN, p % CORES
    l, z = c // ZN, c % ZN
    other = (1 - l) * ZN + z
    up_z, down_z = l * ZN + (z + 1) % ZN, l * ZN + (z + ZN - 1) % ZN
    sibling = p + 1 - 2 * core
    mine = x * CORES + core
    cols = w.shape[1]
    first_chan = p * OWN

    def wcols(slot):
        return wbuf.at[:, pl.ds(pl.multiple_of(slot * cols, cols), cols)]

    loads = [
        pltpu.make_async_copy(src, dst, local.at[i])
        for i, (src, dst) in enumerate(
            [(g, gbuf), (w, wcols(mine)), (q, qkv.at[0]), (k, qkv.at[1]), (v, qkv.at[2]),
             (sw, swv), (res, resv), (ld, ldv)]
        )
    ]
    for copy in loads:
        copy.start()

    barrier = pltpu.get_barrier_semaphore()

    @pl.loop(1, POS)
    def _(i):
        pl.semaphore_signal(barrier, 1, device_id={"pos": (p + i) % POS}, device_id_type=MESH)

    for d in (other, up_z, down_z):
        pl.semaphore_signal(barrier, 1, device_id={"chan": d}, device_id_type=MESH)

    loads[0].wait()
    wide = gbuf[...].astype(F32)
    part = wide.shape[1] // YH
    for i in range(YH):
        at = i * part
        gst[i] = jnp.concatenate(
            [wide[:, at : at + part // 2], wide[:, at + part // 2 : at + part]], axis=0
        ).astype(BF16)
    loads[1].wait()
    pl.semaphore_wait(barrier, POS - 1 + 3)

    xbuf[0, h] = gst[h]

    def piece(r):
        return (h + YH - NEAR[r]) % YH

    def ring(way, sel, hop, r):
        source = (sel, way if hop > 1 else 0, hop - 1)
        to = SLOT[(sel, way, hop)]
        return remote(xbuf.at[SLOT[source], piece(r)], xbuf.at[to, piece(r)],
                      rs.at[to * YH + r], rr.at[to * YH + r],
                      chan=up_z if way == 0 else down_z)

    hops, across = [], []

    def send(way, sel, hop, r):
        hops.append(ring(way, sel, hop, r))
        hops[-1].start()

    def pass_own(r):
        send(0, 0, 1, r)
        send(1, 0, 1, r)
        across.append(remote(xbuf.at[0, piece(r)], xbuf.at[1, piece(r)], ls.at[r], lr.at[r],
                             chan=other))
        across[-1].start()

    first = []
    for i in range(1, YH):
        to = (h + NEAR[i]) % YH
        first.append(remote(gst.at[to], xbuf.at[0, h], gss.at[i - 1], gsr.at[i - 1],
                            pos=to * ROW + x * CORES + core))
        first[-1].start()
    pass_own(0)
    weights = []
    for i in (1, 3, 2):
        to = h * ROW + ((x + i) % XN) * CORES + core
        weights.append(remote(wcols(mine), wcols(mine), ws.at[i - 1], wr.at[i - 1], pos=to))
        weights[-1].start()
    share = remote(wcols(mine), wcols(mine), ws.at[3], wr.at[3], pos=sibling)
    share.start()

    for s in range(3):
        loads[2 + s].wait()
        slab[:, s] = qkv[s].astype(F32).T.astype(BF16).reshape(POS, OWN, BLK)
        first[s].wait_recv()
        pass_own(s + 1)

    @pl.loop(1, POS)
    def _(i):
        to = (p + i) % POS
        remote(slab.at[to], inb.at[p], qs, qr, pos=to).start()

    inb[p] = slab[p]

    shared = []

    def share_weights(i):
        slot = ((x + XN - i) % XN) * CORES + core
        remote(wcols(slot), wcols(slot), ws.at[i - 1], wr.at[i - 1], pos=sibling).wait_recv()
        shared.append(remote(wcols(slot), wcols(slot), ws.at[3 + i], wr.at[3 + i], pos=sibling))
        shared[-1].start()

    def arrive(sel, hop, *work):
        for r in range(YH):
            for way in (0, 1):
                if (sel, way, hop) in SLOT:
                    ring(way, sel, hop, r).wait_recv()
                    if (sel, way, hop + 1) in SLOT:
                        send(way, sel, hop + 1, r)
            if r < len(work):
                work[r]()

    half = xbuf.shape[3]
    rest_slots = pl.ds(0, POS - 1)

    def product(tile):
        both = xbuf[pl.ds(tile * GROUP, GROUP)].astype(F32).reshape(GROUP * YH, 2, 8, half)
        rows = jnp.concatenate(
            [both[:, 0].reshape(BLK, half), both[:, 1].reshape(BLK, half)], axis=1
        ).astype(BF16)
        pout[:, tile] = dot(wbuf[...], rows, 1, 1).astype(BF16).reshape(POS, OWN, BLK)

    def give_part(part):
        tiles = pl.ds(*PARTS[part])

        @pl.loop(1, POS)
        def _(i):
            to = (p + i) % POS
            remote(pout.at[to, tiles], pin.at[p, tiles], ps.at[part], pr.at[part], pos=to).start()

        pin[p, tiles] = pout[p, tiles]

    for r in range(YH):
        across[r].wait_recv()
        send(0, 1, 1, r)
        send(1, 1, 1, r)

    for copy in loads[5:]:
        copy.wait()
    chans = swv.shape[2]
    pick = lax.broadcasted_iota(jnp.int32, (OWN, chans), 1) == (
        first_chan + lax.broadcasted_iota(jnp.int32, (OWN, chans), 0)
    )
    taps_of = [
        [
            jnp.sum(jnp.where(pick, swv[s, pl.ds(j, 1), :], 0.0), axis=1, keepdims=True)[None]
            for j in range(TAPS)
        ]
        for s in range(3)
    ]
    eye = (
        lax.broadcasted_iota(jnp.int32, (OWN, MODES, MODES), 1)
        == lax.broadcasted_iota(jnp.int32, (OWN, MODES, MODES), 2)
    )

    def columns(ref):
        own = pltpu.roll(ref[...], chans - first_chan, 1)[:, :BLK].T[:OWN]
        spread = jnp.where(eye, jnp.broadcast_to(own[:, None, :], eye.shape), 0.0)
        return jnp.sum(spread, axis=2, keepdims=True)

    shape3 = (OWN, MODES, BLK)
    time = lax.broadcasted_iota(jnp.int32, shape3, 2).astype(F32)
    weight = jnp.broadcast_to(columns(resv), shape3)
    rate = jnp.exp(jnp.broadcast_to(columns(ldv), shape3))
    near = jnp.exp(-rate * time)
    ahead = jnp.exp(-rate * (time + 1.0))
    back = jnp.exp(-rate * (BLK - 1.0 - time))
    taps = jnp.sum(weight * near, axis=1)
    t_ahead = (time + 1.0) * ahead
    t_back = (BLK - 1.0 - time) * back
    w_ahead = weight * ahead
    w_back = weight * back

    arrive(0, 1)
    arrive(1, 1)
    blocks = POS
    rows = blocks * OWN
    shape = (blocks, OWN, BLK)
    row2 = lax.broadcasted_iota(jnp.int32, (BLK, BLK), 0)
    lane2 = lax.broadcasted_iota(jnp.int32, (BLK, BLK), 1)
    fill = jnp.zeros((BLK - blocks, BLK), F32)
    held = {}

    def stream(s):
        return inb[:, s].astype(F32)

    def conv(s):
        values = stream(s)
        return sum(taps_of[s][j] * later(values, j) for j in range(TAPS))

    def strided(i):
        return pl.ds(i, blocks, stride=OWN)

    def gate():
        remote(slab.at[rest_slots], inb.at[rest_slots], qs, qr, pos=sibling).wait()
        xs[...] = (conv(1) * conv(2)).astype(BF16).astype(F32).reshape(rows, BLK)

    def within(low, high):
        def work():
            for i in range(low, high):
                gated = xs[strided(i), :]
                turned = pltpu.roll(
                    jnp.broadcast_to(taps[i : i + 1], (BLK, BLK)), 0, 1, stride=1, stride_axis=0
                )
                toep[i] = jnp.where(lane2 >= row2, turned, 0.0).astype(BF16)
                fs[pl.ds(i * blocks, blocks), :] = dot(gated.astype(BF16), toep[i], 1, 0)
                up[i] = dot(
                    jnp.concatenate([*halves(back[i]), *halves(t_back[i])], axis=0),
                    jnp.concatenate([gated, fill], axis=0).astype(BF16), 1, 1,
                )
        return work

    n = MODES

    def edges():
        flip = (row2 + lane2 == BLK - 1).astype(F32).astype(BF16)
        xr[...] = dot(xs[...].astype(BF16), flip, 1, 0)
        s0 = up[:, 0:n] + up[:, n : 2 * n]
        s1 = up[:, 2 * n : 3 * n] + up[:, 3 * n : 4 * n]
        held["falls"] = falls = []
        for e in range(5):
            skip = 1 << e
            falls.append(jnp.exp(-rate * float(BLK * skip)))
            s0_k = pltpu.roll(s0, skip, 2)
            s1 = s1 + falls[e] * (pltpu.roll(s1, skip, 2) + float(BLK * skip) * s0_k)
            s0 = s0 + falls[e] * s0_k
        held["state"], held["d_state"] = pltpu.roll(s0, 1, 2), pltpu.roll(s1, 1, 2)

    def between(low, high):
        def work():
            for i in range(low, high):
                xs[strided(i), :] = (
                    fs[pl.ds(i * blocks, blocks), :]
                    + joined(held["state"][i], w_ahead[i])[:blocks]
                )
        return work

    lanes = GROUPS * BLK
    each = BLK // GROUP

    def order():
        row_p = lax.broadcasted_iota(jnp.int32, (each, lanes), 0)
        lane_p = lax.broadcasted_iota(jnp.int32, (each, lanes), 1)
        for i, (sel, way, hop) in enumerate(ORDER):
            chip = (z + ZN - hop) % ZN if way == 0 else (z + hop) % ZN
            chunk = (l if sel == 0 else 1 - l) * ZN + chip
            goes = (row_p // 8) * BLK + chunk * 8 + row_p % 8
            perm[pl.ds(i * each, each), :] = (lane_p == goes).astype(F32).astype(BF16)

    def weights_in():
        share.wait_recv()
        for copy in shared:
            copy.wait_recv()
        product(0)

    half_own = OWN // 2
    arrive(0, 2)
    for i in (1, 3, 2):
        share_weights(i)
    arrive(1, 2, weights_in, lambda: product(1), lambda: give_part(0))
    arrive(0, 3, order)
    arrive(1, 3)
    product(2)
    give_part(1)
    gate()
    within(0, OWN)()
    edges()
    between(0, OWN)()
    for r in range(YH):
        for sel, way, hop in ORDER[-2:]:
            ring(way, sel, hop, r).wait_recv()
    product(3)
    give_part(2)
    falls, state, d_state = held["falls"], held["state"], held["d_state"]

    own_rows = ROW * OWN
    tiles = []
    for part, (first_tile, count) in enumerate(PARTS):
        some = (rest_slots, pl.ds(first_tile, count))
        remote(pout.at[some], pin.at[some], ps.at[part], pr.at[part], pos=sibling).wait()
        for i in range(first_tile, first_tile + count):
            total = sum(pin[pl.ds(j * ROW, ROW), i].astype(F32) for j in range(YH))
            tiles.append(total.reshape(own_rows, BLK).astype(BF16))
    ordered = dot(jnp.concatenate(tiles, axis=1), perm[...], 1, 0)
    mix = jnp.concatenate(
        [ordered[:, i * BLK : (i + 1) * BLK].reshape(ROW, OWN, BLK) for i in range(YH)], axis=0
    )

    lane = lax.broadcasted_iota(jnp.int32, (OWN, BLK), 1)
    sums = []

    def finish_stream(s, grad, ref, index):
        values = stream(s)
        total = sum(taps_of[s][j] * sooner(grad, j) for j in range(TAPS)).astype(BF16)
        if index is None:
            ref[...] = total
        else:
            ref[:, index] = total
        for j in range(TAPS):
            sums.append(jnp.sum(grad * later(values, j), axis=0))

    def give(mine_ref, all_ref, sem, *index):
        @pl.loop(1, POS)
        def _(i):
            to = (p + i) % POS
            remote(mine_ref.at[(to, *index)], all_ref.at[(p, *index)], os.at[sem], orr.at[sem],
                   pos=to).start()

        all_ref[(p, *index)] = mine_ref[(p, *index)]

    finish_stream(0, mix * xs[...].reshape(shape), gqs, None)
    give(gqs, gqb, 0)

    gs[...] = (mix * conv(0).astype(BF16).astype(F32)).astype(BF16).astype(F32).reshape(rows, BLK)
    for i in range(OWN):
        grad = gs[strided(i), :]
        low = grad.astype(BF16)
        gg[pl.ds(i * blocks, blocks), :] = dot(low, toep[i], 1, 1)
        vp[i] = dot(
            jnp.concatenate([*halves(ahead[i]), *halves(t_ahead[i])], axis=0),
            jnp.concatenate([grad, fill], axis=0).astype(BF16), 1, 1,
        )
    t0, t1 = vp[:, 0:n] + vp[:, n : 2 * n], vp[:, 2 * n : 3 * n] + vp[:, 3 * n : 4 * n]
    rest = t0
    for e in range(5):
        rest = rest + falls[e] * pltpu.roll(rest, BLK - (1 << e), 2)
    rest = pltpu.roll(rest, BLK - 1, 2)
    for i in range(OWN):
        xs[strided(i), :] = (
            gg[pl.ds(i * blocks, blocks), :] + joined(rest[i], w_back[i])[:blocks]
        )
    grad_gated = xs[...].reshape(shape)
    finish_stream(1, grad_gated * conv(2), gkvs, 0)
    give(gkvs, gkvb, 1, 0)
    finish_stream(2, grad_gated * conv(1), gkvs, 1)

    for i in range(OWN):
        pair = dot(xr[strided(i), :].astype(BF16), gs[strided(i), :].astype(BF16), 0, 0)
        turned = pltpu.roll(pair, 1, 1, stride=1, stride_axis=0)
        cd[pl.ds(i, 1), :] = jnp.sum(jnp.where(lane2 <= row2, turned, 0.0), axis=0, keepdims=True)
    corr = cd[...][:, None, :] * near
    by_res = jnp.sum(corr + t0 * state, axis=2, keepdims=True)
    by_rate = jnp.sum(corr * time + t1 * state + t0 * d_state, axis=2, keepdims=True)
    by_log = -by_rate * weight * rate
    lane3 = lax.broadcasted_iota(jnp.int32, shape3, 2)
    mode3 = lax.broadcasted_iota(jnp.int32, shape3, 1)
    tiny = jnp.sum(
        jnp.where(lane3 == 16 + mode3, by_res, jnp.where(lane3 == 32 + mode3, by_log, 0.0)), axis=1
    )
    for j, total in enumerate(sums):
        tiny = jnp.where(lane == j, jnp.sum(total, axis=1, keepdims=True), tiny)
    smalls[...] = jnp.where(lane[:8] < BLK // 2, tiny[:8], pltpu.roll(tiny[8:], BLK // 2, 1))

    for i in range(1, YH):
        to = ((h + i) % YH) * ROW + mine
        remote(smalls, smallb.at[mine, h], os.at[3], orr.at[3], pos=to).start()
    smallb[mine, h] = smalls[...]
    give(gkvs, gkvb, 2, 1)
    three = smallb.at[0, pl.ds(0, YH - 1)]
    remote(three, three, os.at[3], orr.at[3], pos=sibling).wait()

    @pl.loop(1, ROW)
    def _(i):
        to = h * ROW + (mine + i) % ROW
        remote(smallb.at[mine], smallb.at[mine], os.at[4], orr.at[4], pos=to).start()

    for copy in first + weights + [share] + across + hops + shared:
        copy.wait_send()
    gkv_rest = [gkvb.at[rest_slots, i] for i in (0, 1)]
    for sem, ref in enumerate((gqb.at[rest_slots], *gkv_rest)):
        remote(ref, ref, os.at[sem], orr.at[sem], pos=sibling).wait()
    gq_out[...] = gqb[...]
    gkv_out[...] = gkvb[...]
    seven = smallb.at[pl.ds(0, ROW - 1)]
    remote(seven, seven, os.at[4], orr.at[4], pos=sibling).wait()
    small_out[...] = smallb[...]


def mixer(q, k, v, short_weights, residues, log_decay, w, g):
    chans, cols = w.shape
    dma = pltpu.SemaphoreType.DMA
    half = g.shape[1] // YH // 2
    rows = POS * OWN
    outs = [((POS, OWN, BLK), BF16), ((POS, 2, OWN, BLK), BF16), ((ROW, YH, 8, BLK), F32)]
    return pl.pallas_call(
        mixer_kernel,
        out_shape=tuple(jax.ShapeDtypeStruct(*o) for o in outs),
        in_specs=[full(pl.ANY)] * 8,
        out_specs=(full(),) * 3,
        scratch_shapes=[
            pltpu.VMEM((3, BLK, chans), BF16),
            pltpu.VMEM(g.shape, BF16),
            pltpu.VMEM(short_weights.shape, F32),
            pltpu.VMEM(residues.shape, F32),
            pltpu.VMEM(log_decay.shape, F32),
            pltpu.VMEM((POS, 3, OWN, BLK), BF16),
            pltpu.VMEM((POS, 3, OWN, BLK), BF16),
            pltpu.VMEM((chans, ROW * cols), BF16),
            pltpu.VMEM((YH, 16, half), BF16),
            pltpu.VMEM((CHAN, YH, 16, half), BF16),
            pltpu.VMEM((POS, GROUPS, OWN, BLK), BF16),
            pltpu.VMEM((POS, GROUPS, OWN, BLK), BF16),
            pltpu.VMEM((GROUPS * BLK, GROUPS * BLK), BF16),
        ]
        + [pltpu.VMEM((rows, BLK), F32)] * 5
        + [pltpu.VMEM((OWN, 4 * MODES, BLK), F32)] * 2
        + [pltpu.VMEM((OWN, BLK), F32), pltpu.VMEM((OWN, BLK, BLK), BF16)]
        + [pltpu.VMEM(*o) for o in (outs[0], outs[1], outs[0], outs[1])]
        + [pltpu.VMEM((8, BLK), F32), pltpu.VMEM(*outs[2])]
        + [
            dma((8,)),
            dma, dma,
            dma((YH - 1,)), dma((YH - 1,)),
            dma((7,)), dma((7,)),
            dma((YH,)), dma((YH,)),
            dma((CHAN * YH,)), dma((CHAN * YH,)),
            dma((len(PARTS),)), dma((len(PARTS),)),
            dma((5,)), dma((5,)),
        ],
        compiler_params=pltpu.CompilerParams(
            collective_id=0, has_side_effects=True, vmem_limit_bytes=VMEM
        ),
        name="mixer",
    )(q, k, v, short_weights, residues, log_decay, w, g)


def finish_kernel(gq_in, gkv_in, small_in, q, k, v, short, res, dec, gq, gkv, small, local):
    chans = POS * OWN
    loads = [
        pltpu.make_async_copy(src, dst, local.at[i])
        for i, (src, dst) in enumerate([(gq_in, gq), (gkv_in, gkv), (small_in, small)])
    ]
    for copy in loads:
        copy.start()
    loads[0].wait()
    q[...] = gq[...].astype(F32).reshape(chans, BLK).T.astype(BF16)
    loads[1].wait()
    for s, ref in enumerate((k, v)):
        ref[...] = gkv[:, s].astype(F32).reshape(chans, BLK).T.astype(BF16)
    loads[2].wait()
    packed = small[...]
    both = jnp.concatenate([packed, pltpu.roll(packed, BLK // 2, 3)], axis=2)
    turned = jnp.concatenate([both[:, i] for i in range(YH)], axis=0).reshape(chans, BLK).T
    res[...] = turned[16:32]
    dec[...] = turned[32:48]
    for s in range(3):
        short[s] = turned[s * TAPS : (s + 1) * TAPS]


def finish(gq, gkv, small):
    chans = POS * OWN
    stream = jax.ShapeDtypeStruct((BLK, chans), BF16)
    mode = jax.ShapeDtypeStruct((MODES, chans), F32)
    return pl.pallas_call(
        finish_kernel,
        out_shape=(stream, stream, stream, jax.ShapeDtypeStruct((3, TAPS, chans), F32), mode, mode),
        in_specs=[full(pl.ANY)] * 3,
        out_specs=(full(),) * 6,
        scratch_shapes=[pltpu.VMEM(a.shape, a.dtype) for a in (gq, gkv, small)]
        + [pltpu.SemaphoreType.DMA((3,))],
        compiler_params=pltpu.CompilerParams(vmem_limit_bytes=VMEM),
        name="finish",
    )(gq, gkv, small)


def local(q_in, k_in, v_in, short_weights, residues, log_decay, out_weight, grad_out):
    parts = mixer(
        q_in, k_in, v_in, short_weights, residues.T, log_decay.T, out_weight, grad_out
    )
    gq, gk, gv, short, res, dec = finish(*parts)
    return gq, gk, gv, short, res.T, dec.T


def solution(mesh):
    in_specs = (
        P("pos", "chan"),
        P("pos", "chan"),
        P("pos", "chan"),
        P(None, None, "chan"),
        P("chan", None),
        P("chan", None),
        P("chan", "pos"),
        P(("pos", "chan"), None),
    )
    out_specs = (
        P("pos", "chan"),
        P("pos", "chan"),
        P("pos", "chan"),
        P(None, None, "chan"),
        P("chan", None),
        P("chan", None),
    )
    return jax.shard_map(local, mesh=mesh, in_specs=in_specs, out_specs=out_specs, check_vma=False)
```

```python
import functools

import jax
import jax.numpy as jnp
from jax import lax
from jax.experimental import pallas as pl
from jax.experimental.pallas import tpu as pltpu
from jax.sharding import PartitionSpec as P

F32 = jnp.float32
BF16 = jnp.bfloat16
MESH = pl.DeviceIdType.MESH

YH, XN, CORES = 4, 4, 2
YL, ZN = 2, 8
POS = YH * XN * CORES
CHAN = YL * ZN
ROW = XN * CORES
BLK = 128
OWN = 16
MODES = 16
TAPS = 3
VMEM = 60 * 1024 * 1024


def remote(src, dst, send, recv, **device):
    return pltpu.make_async_remote_copy(
        src_ref=src, dst_ref=dst, send_sem=send, recv_sem=recv,
        device_id=device, device_id_type=MESH,
    )


def full(memory=pltpu.VMEM):
    return pl.BlockSpec(memory_space=memory)


def later(x, j):
    if j == 0:
        return x
    lane = lax.broadcasted_iota(jnp.int32, x.shape, 2)
    turned = pltpu.roll(x, j, 2)
    before = jnp.concatenate([jnp.zeros_like(turned[:1]), turned[:-1]], axis=0)
    return jnp.where(lane < j, before, turned)


def sooner(x, j):
    if j == 0:
        return x
    lane = lax.broadcasted_iota(jnp.int32, x.shape, 2)
    turned = pltpu.roll(x, BLK - j, 2)
    after = jnp.concatenate([turned[1:], jnp.zeros_like(turned[:1])], axis=0)
    return jnp.where(lane >= BLK - j, after, turned)


def halves(x):
    high = x.astype(BF16)
    return high, (x - high.astype(F32)).astype(BF16)


def dot(a, b, da, db):
    return lax.dot_general(a, b, (((da,), (db,)), ((), ())), preferred_element_type=F32)


def joined(states, table):
    sh, sl = halves(states)
    th, tl = halves(table)
    return dot(jnp.concatenate([sh, sh, sl], axis=0), jnp.concatenate([th, tl, th], axis=0), 0, 0)


ORDER = [(0, 0, 0), (1, 0, 0)]
for hop in range(1, ZN // 2):
    ORDER += [(0, 0, hop), (0, 1, hop), (1, 0, hop), (1, 1, hop)]
ORDER += [(0, 0, ZN // 2), (1, 1, ZN // 2)]
SLOT = {key: i for i, key in enumerate(ORDER)}
NEAR = (0, 1, 3, 2)
GROUP = 4
GROUPS = CHAN // GROUP
PARTS = ((0, 2), (2, 1), (3, 1))


def mixer_kernel(
    q, k, v, sw, res, ld, w, g, gq_out, gkv_out, small_out,
    qkv, gbuf, swv, resv, ldv, slab, inb, wbuf, gst, xbuf, pout, pin, perm,
    xs, xr, gs, fs, gg, up, vp, cd, toep, gqs, gkvs, gqb, gkvb, smalls, smallb,
    local, qs, qr, gss, gsr, ws, wr, ls, lr, rs, rr, ps, pr, os, orr,
):
    p = lax.axis_index("pos")
    c = lax.axis_index("chan")
    h, x, core = p // ROW, (p // CORES) % XN, p % CORES
    l, z = c // ZN, c % ZN
    other = (1 - l) * ZN + z
    up_z, down_z = l * ZN + (z + 1) % ZN, l * ZN + (z + ZN - 1) % ZN
    sibling = p + 1 - 2 * core
    mine = x * CORES + core
    cols = w.shape[1]
    first_chan = p * OWN

    def wcols(slot):
        return wbuf.at[:, pl.ds(pl.multiple_of(slot * cols, cols), cols)]

    loads = [
        pltpu.make_async_copy(src, dst, local.at[i])
        for i, (src, dst) in enumerate(
            [(g, gbuf), (w, wcols(mine)), (q, qkv.at[0]), (k, qkv.at[1]), (v, qkv.at[2]),
             (sw, swv), (res, resv), (ld, ldv)]
        )
    ]
    for copy in loads:
        copy.start()

    barrier = pltpu.get_barrier_semaphore()

    @pl.loop(1, POS)
    def _(i):
        pl.semaphore_signal(barrier, 1, device_id={"pos": (p + i) % POS}, device_id_type=MESH)

    for d in (other, up_z, down_z):
        pl.semaphore_signal(barrier, 1, device_id={"chan": d}, device_id_type=MESH)

    loads[0].wait()
    wide = gbuf[...].astype(F32)
    part = wide.shape[1] // YH
    for i in range(YH):
        at = i * part
        gst[i] = jnp.concatenate(
            [wide[:, at : at + part // 2], wide[:, at + part // 2 : at + part]], axis=0
        ).astype(BF16)
    loads[1].wait()
    pl.semaphore_wait(barrier, POS - 1 + 3)

    xbuf[0, h] = gst[h]

    def piece(r):
        return (h + YH - NEAR[r]) % YH

    def ring(way, sel, hop, r):
        source = (sel, way if hop > 1 else 0, hop - 1)
        to = SLOT[(sel, way, hop)]
        return remote(xbuf.at[SLOT[source], piece(r)], xbuf.at[to, piece(r)],
                      rs.at[to * YH + r], rr.at[to * YH + r],
                      chan=up_z if way == 0 else down_z)

    hops, across = [], []

    def send(way, sel, hop, r):
        hops.append(ring(way, sel, hop, r))
        hops[-1].start()

    def pass_own(r):
        send(0, 0, 1, r)
        send(1, 0, 1, r)
        across.append(remote(xbuf.at[0, piece(r)], xbuf.at[1, piece(r)], ls.at[r], lr.at[r],
                             chan=other))
        across[-1].start()

    first = []
    for i in range(1, YH):
        to = (h + NEAR[i]) % YH
        first.append(remote(gst.at[to], xbuf.at[0, h], gss.at[i - 1], gsr.at[i - 1],
                            pos=to * ROW + x * CORES + core))
        first[-1].start()
    pass_own(0)
    weights = []
    for i in (1, 3, 2):
        to = h * ROW + ((x + i) % XN) * CORES + core
        weights.append(remote(wcols(mine), wcols(mine), ws.at[i - 1], wr.at[i - 1], pos=to))
        weights[-1].start()
    share = remote(wcols(mine), wcols(mine), ws.at[3], wr.at[3], pos=sibling)
    share.start()

    for s in range(3):
        loads[2 + s].wait()
        slab[:, s] = qkv[s].astype(F32).T.astype(BF16).reshape(POS, OWN, BLK)
        first[s].wait_recv()
        pass_own(s + 1)

    shared = []

    def share_weights(i):
        slot = ((x + XN - i) % XN) * CORES + core
        remote(wcols(slot), wcols(slot), ws.at[i - 1], wr.at[i - 1], pos=sibling).wait_recv()
        shared.append(remote(wcols(slot), wcols(slot), ws.at[3 + i], wr.at[3 + i], pos=sibling))
        shared[-1].start()

    def arrive(sel, hop, *work):
        for r in range(YH):
            for way in (0, 1):
                if (sel, way, hop) in SLOT:
                    ring(way, sel, hop, r).wait_recv()
                    if (sel, way, hop + 1) in SLOT:
                        send(way, sel, hop + 1, r)
            if r < len(work):
                work[r]()

    half = xbuf.shape[3]
    rest_slots = pl.ds(0, POS - 1)

    def product(tile):
        both = xbuf[pl.ds(tile * GROUP, GROUP)].astype(F32).reshape(GROUP * YH, 2, 8, half)
        rows = jnp.concatenate(
            [both[:, 0].reshape(BLK, half), both[:, 1].reshape(BLK, half)], axis=1
        ).astype(BF16)
        pout[:, tile] = dot(wbuf[...], rows, 1, 1).astype(BF16).reshape(POS, OWN, BLK)

    def give_part(part):
        tiles = pl.ds(*PARTS[part])

        @pl.loop(1, POS)
        def _(i):
            to = (p + (i + 7) % (POS - 1) + 1) % POS
            remote(pout.at[to, tiles], pin.at[p, tiles], ps.at[part], pr.at[part], pos=to).start()

        pin[p, tiles] = pout[p, tiles]

    for r in range(YH):
        across[r].wait_recv()
        send(0, 1, 1, r)
        send(1, 1, 1, r)

    @pl.loop(1, POS)
    def _(i):
        to = (p + i) % POS
        remote(slab.at[to], inb.at[p], qs, qr, pos=to).start()

    inb[p] = slab[p]

    arrive(0, 1)
    arrive(1, 1)
    blocks = POS
    rows = blocks * OWN
    shape = (blocks, OWN, BLK)
    row2 = lax.broadcasted_iota(jnp.int32, (BLK, BLK), 0)
    lane2 = lax.broadcasted_iota(jnp.int32, (BLK, BLK), 1)
    fill = jnp.zeros((BLK - blocks, BLK), F32)
    held = {}

    def stream(s):
        return inb[:, s].astype(F32)

    def conv(s):
        values = stream(s)
        return sum(taps_of[s][j] * later(values, j) for j in range(TAPS))

    def strided(i):
        return pl.ds(i, blocks, stride=OWN)

    def gate():
        remote(slab.at[rest_slots], inb.at[rest_slots], qs, qr, pos=sibling).wait()
        xs[...] = (conv(1) * conv(2)).astype(BF16).astype(F32).reshape(rows, BLK)

    def within(low, high):
        def work():
            for i in range(low, high):
                gated = xs[strided(i), :]
                turned = pltpu.roll(
                    jnp.broadcast_to(taps[i : i + 1], (BLK, BLK)), 0, 1, stride=1, stride_axis=0
                )
                toep[i] = jnp.where(lane2 >= row2, turned, 0.0).astype(BF16)
                fs[pl.ds(i * blocks, blocks), :] = dot(gated.astype(BF16), toep[i], 1, 0)
                up[i] = dot(
                    jnp.concatenate([*halves(back[i]), *halves(t_back[i])], axis=0),
                    jnp.concatenate([gated, fill], axis=0).astype(BF16), 1, 1,
                )
        return work

    n = MODES

    def edges():
        flip = (row2 + lane2 == BLK - 1).astype(F32).astype(BF16)
        xr[...] = dot(xs[...].astype(BF16), flip, 1, 0)
        s0 = up[:, 0:n] + up[:, n : 2 * n]
        s1 = up[:, 2 * n : 3 * n] + up[:, 3 * n : 4 * n]
        held["falls"] = falls = []
        for e in range(5):
            skip = 1 << e
            falls.append(jnp.exp(-rate * float(BLK * skip)))
            s0_k = pltpu.roll(s0, skip, 2)
            s1 = s1 + falls[e] * (pltpu.roll(s1, skip, 2) + float(BLK * skip) * s0_k)
            s0 = s0 + falls[e] * s0_k
        held["state"], held["d_state"] = pltpu.roll(s0, 1, 2), pltpu.roll(s1, 1, 2)

    def between(low, high):
        def work():
            for i in range(low, high):
                xs[strided(i), :] = (
                    fs[pl.ds(i * blocks, blocks), :]
                    + joined(held["state"][i], w_ahead[i])[:blocks]
                )
        return work

    lanes = GROUPS * BLK
    each = BLK // GROUP

    def order():
        row_p = lax.broadcasted_iota(jnp.int32, (each, lanes), 0)
        lane_p = lax.broadcasted_iota(jnp.int32, (each, lanes), 1)
        for i, (sel, way, hop) in enumerate(ORDER):
            chip = (z + ZN - hop) % ZN if way == 0 else (z + hop) % ZN
            chunk = (l if sel == 0 else 1 - l) * ZN + chip
            goes = (row_p // 8) * BLK + chunk * 8 + row_p % 8
            perm[pl.ds(i * each, each), :] = (lane_p == goes).astype(F32).astype(BF16)

    def weights_in():
        share.wait_recv()
        for copy in shared:
            copy.wait_recv()
        product(0)

    half_own = OWN // 2
    arrive(0, 2)
    for i in (1, 3, 2):
        share_weights(i)
    arrive(1, 2)
    arrive(0, 3, weights_in, lambda: product(1), lambda: give_part(0), order)
    arrive(1, 3)
    product(2)
    give_part(1)

    for copy in loads[5:]:
        copy.wait()
    chans = swv.shape[2]
    pick = lax.broadcasted_iota(jnp.int32, (OWN, chans), 1) == (
        first_chan + lax.broadcasted_iota(jnp.int32, (OWN, chans), 0)
    )
    taps_of = [
        [
            jnp.sum(jnp.where(pick, swv[s, pl.ds(j, 1), :], 0.0), axis=1, keepdims=True)[None]
            for j in range(TAPS)
        ]
        for s in range(3)
    ]
    eye = (
        lax.broadcasted_iota(jnp.int32, (OWN, MODES, MODES), 1)
        == lax.broadcasted_iota(jnp.int32, (OWN, MODES, MODES), 2)
    )

    def columns(ref):
        own = pltpu.roll(ref[...], chans - first_chan, 1)[:, :BLK].T[:OWN]
        spread = jnp.where(eye, jnp.broadcast_to(own[:, None, :], eye.shape), 0.0)
        return jnp.sum(spread, axis=2, keepdims=True)

    shape3 = (OWN, MODES, BLK)
    time = lax.broadcasted_iota(jnp.int32, shape3, 2).astype(F32)
    weight = jnp.broadcast_to(columns(resv), shape3)
    rate = jnp.exp(jnp.broadcast_to(columns(ldv), shape3))
    near = jnp.exp(-rate * time)
    ahead = jnp.exp(-rate * (time + 1.0))
    back = jnp.exp(-rate * (BLK - 1.0 - time))
    taps = jnp.sum(weight * near, axis=1)
    t_ahead = (time + 1.0) * ahead
    t_back = (BLK - 1.0 - time) * back
    w_ahead = weight * ahead
    w_back = weight * back

    gate()
    within(0, OWN)()
    edges()
    between(0, OWN)()
    for r in range(YH):
        for sel, way, hop in ORDER[-2:]:
            ring(way, sel, hop, r).wait_recv()
    product(3)
    give_part(2)
    falls, state, d_state = held["falls"], held["state"], held["d_state"]

    own_rows = ROW * OWN
    tiles = []
    for part, (first_tile, count) in enumerate(PARTS):
        some = (rest_slots, pl.ds(first_tile, count))
        remote(pout.at[some], pin.at[some], ps.at[part], pr.at[part], pos=sibling).wait()
        for i in range(first_tile, first_tile + count):
            total = sum(pin[pl.ds(j * ROW, ROW), i].astype(F32) for j in range(YH))
            tiles.append(total.reshape(own_rows, BLK).astype(BF16))
    ordered = dot(jnp.concatenate(tiles, axis=1), perm[...], 1, 0)
    mix = jnp.concatenate(
        [ordered[:, i * BLK : (i + 1) * BLK].reshape(ROW, OWN, BLK) for i in range(YH)], axis=0
    )

    lane = lax.broadcasted_iota(jnp.int32, (OWN, BLK), 1)
    sums = []

    def finish_stream(s, grad, ref, index):
        values = stream(s)
        total = sum(taps_of[s][j] * sooner(grad, j) for j in range(TAPS)).astype(BF16)
        if index is None:
            ref[...] = total
        else:
            ref[:, index] = total
        for j in range(TAPS):
            sums.append(jnp.sum(grad * later(values, j), axis=0))

    def give(mine_ref, all_ref, sem, *index):
        @pl.loop(1, POS)
        def _(i):
            to = (p + (i + 7) % (POS - 1) + 1) % POS
            remote(mine_ref.at[(to, *index)], all_ref.at[(p, *index)], os.at[sem], orr.at[sem],
                   pos=to).start()

        all_ref[(p, *index)] = mine_ref[(p, *index)]

    finish_stream(0, mix * xs[...].reshape(shape), gqs, None)
    give(gqs, gqb, 0)

    gs[...] = (mix * conv(0).astype(BF16).astype(F32)).astype(BF16).astype(F32).reshape(rows, BLK)
    for i in range(OWN):
        grad = gs[strided(i), :]
        low = grad.astype(BF16)
        gg[pl.ds(i * blocks, blocks), :] = dot(low, toep[i], 1, 1)
        vp[i] = dot(
            jnp.concatenate([*halves(ahead[i]), *halves(t_ahead[i])], axis=0),
            jnp.concatenate([grad, fill], axis=0).astype(BF16), 1, 1,
        )
    t0, t1 = vp[:, 0:n] + vp[:, n : 2 * n], vp[:, 2 * n : 3 * n] + vp[:, 3 * n : 4 * n]
    rest = t0
    for e in range(5):
        rest = rest + falls[e] * pltpu.roll(rest, BLK - (1 << e), 2)
    rest = pltpu.roll(rest, BLK - 1, 2)
    for i in range(OWN):
        xs[strided(i), :] = (
            gg[pl.ds(i * blocks, blocks), :] + joined(rest[i], w_back[i])[:blocks]
        )
    grad_gated = xs[...].reshape(shape)
    finish_stream(1, grad_gated * conv(2), gkvs, 0)
    give(gkvs, gkvb, 1, 0)
    finish_stream(2, grad_gated * conv(1), gkvs, 1)

    for i in range(OWN):
        pair = dot(xr[strided(i), :].astype(BF16), gs[strided(i), :].astype(BF16), 0, 0)
        turned = pltpu.roll(pair, 1, 1, stride=1, stride_axis=0)
        cd[pl.ds(i, 1), :] = jnp.sum(jnp.where(lane2 <= row2, turned, 0.0), axis=0, keepdims=True)
    corr = cd[...][:, None, :] * near
    by_res = jnp.sum(corr + t0 * state, axis=2, keepdims=True)
    by_rate = jnp.sum(corr * time + t1 * state + t0 * d_state, axis=2, keepdims=True)
    by_log = -by_rate * weight * rate
    lane3 = lax.broadcasted_iota(jnp.int32, shape3, 2)
    mode3 = lax.broadcasted_iota(jnp.int32, shape3, 1)
    tiny = jnp.sum(
        jnp.where(lane3 == 16 + mode3, by_res, jnp.where(lane3 == 32 + mode3, by_log, 0.0)), axis=1
    )
    for j, total in enumerate(sums):
        tiny = jnp.where(lane == j, jnp.sum(total, axis=1, keepdims=True), tiny)
    smalls[...] = jnp.where(lane[:8] < BLK // 2, tiny[:8], pltpu.roll(tiny[8:], BLK // 2, 1))

    for i in range(1, YH):
        to = ((h + i) % YH) * ROW + mine
        remote(smalls, smallb.at[mine, h], os.at[3], orr.at[3], pos=to).start()
    smallb[mine, h] = smalls[...]
    give(gkvs, gkvb, 2, 1)
    three = smallb.at[0, pl.ds(0, YH - 1)]
    remote(three, three, os.at[3], orr.at[3], pos=sibling).wait()

    @pl.loop(1, ROW)
    def _(i):
        to = h * ROW + (mine + i) % ROW
        remote(smallb.at[mine], smallb.at[mine], os.at[4], orr.at[4], pos=to).start()

    for copy in first + weights + [share] + across + hops + shared:
        copy.wait_send()
    gkv_rest = [gkvb.at[rest_slots, i] for i in (0, 1)]
    for sem, ref in enumerate((gqb.at[rest_slots], *gkv_rest)):
        remote(ref, ref, os.at[sem], orr.at[sem], pos=sibling).wait()
    gq_out[...] = gqb[...]
    gkv_out[...] = gkvb[...]
    seven = smallb.at[pl.ds(0, ROW - 1)]
    remote(seven, seven, os.at[4], orr.at[4], pos=sibling).wait()
    small_out[...] = smallb[...]


def mixer(q, k, v, short_weights, residues, log_decay, w, g):
    chans, cols = w.shape
    dma = pltpu.SemaphoreType.DMA
    half = g.shape[1] // YH // 2
    rows = POS * OWN
    outs = [((POS, OWN, BLK), BF16), ((POS, 2, OWN, BLK), BF16), ((ROW, YH, 8, BLK), F32)]
    return pl.pallas_call(
        mixer_kernel,
        out_shape=tuple(jax.ShapeDtypeStruct(*o) for o in outs),
        in_specs=[full(pl.ANY)] * 8,
        out_specs=(full(),) * 3,
        scratch_shapes=[
            pltpu.VMEM((3, BLK, chans), BF16),
            pltpu.VMEM(g.shape, BF16),
            pltpu.VMEM(short_weights.shape, F32),
            pltpu.VMEM(residues.shape, F32),
            pltpu.VMEM(log_decay.shape, F32),
            pltpu.VMEM((POS, 3, OWN, BLK), BF16),
            pltpu.VMEM((POS, 3, OWN, BLK), BF16),
            pltpu.VMEM((chans, ROW * cols), BF16),
            pltpu.VMEM((YH, 16, half), BF16),
            pltpu.VMEM((CHAN, YH, 16, half), BF16),
            pltpu.VMEM((POS, GROUPS, OWN, BLK), BF16),
            pltpu.VMEM((POS, GROUPS, OWN, BLK), BF16),
            pltpu.VMEM((GROUPS * BLK, GROUPS * BLK), BF16),
        ]
        + [pltpu.VMEM((rows, BLK), F32)] * 5
        + [pltpu.VMEM((OWN, 4 * MODES, BLK), F32)] * 2
        + [pltpu.VMEM((OWN, BLK), F32), pltpu.VMEM((OWN, BLK, BLK), BF16)]
        + [pltpu.VMEM(*o) for o in (outs[0], outs[1], outs[0], outs[1])]
        + [pltpu.VMEM((8, BLK), F32), pltpu.VMEM(*outs[2])]
        + [
            dma((8,)),
            dma, dma,
            dma((YH - 1,)), dma((YH - 1,)),
            dma((7,)), dma((7,)),
            dma((YH,)), dma((YH,)),
            dma((CHAN * YH,)), dma((CHAN * YH,)),
            dma((len(PARTS),)), dma((len(PARTS),)),
            dma((5,)), dma((5,)),
        ],
        compiler_params=pltpu.CompilerParams(
            collective_id=0, has_side_effects=True, vmem_limit_bytes=VMEM
        ),
        name="mixer",
    )(q, k, v, short_weights, residues, log_decay, w, g)


def finish_kernel(gq_in, gkv_in, small_in, q, k, v, short, res, dec, gq, gkv, small, local):
    chans = POS * OWN
    loads = [
        pltpu.make_async_copy(src, dst, local.at[i])
        for i, (src, dst) in enumerate([(gq_in, gq), (gkv_in, gkv), (small_in, small)])
    ]
    for copy in loads:
        copy.start()
    loads[0].wait()
    q[...] = gq[...].astype(F32).reshape(chans, BLK).T.astype(BF16)
    loads[1].wait()
    for s, ref in enumerate((k, v)):
        ref[...] = gkv[:, s].astype(F32).reshape(chans, BLK).T.astype(BF16)
    loads[2].wait()
    packed = small[...]
    both = jnp.concatenate([packed, pltpu.roll(packed, BLK // 2, 3)], axis=2)
    turned = jnp.concatenate([both[:, i] for i in range(YH)], axis=0).reshape(chans, BLK).T
    res[...] = turned[16:32]
    dec[...] = turned[32:48]
    for s in range(3):
        short[s] = turned[s * TAPS : (s + 1) * TAPS]


def finish(gq, gkv, small):
    chans = POS * OWN
    stream = jax.ShapeDtypeStruct((BLK, chans), BF16)
    mode = jax.ShapeDtypeStruct((MODES, chans), F32)
    return pl.pallas_call(
        finish_kernel,
        out_shape=(stream, stream, stream, jax.ShapeDtypeStruct((3, TAPS, chans), F32), mode, mode),
        in_specs=[full(pl.ANY)] * 3,
        out_specs=(full(),) * 6,
        scratch_shapes=[pltpu.VMEM(a.shape, a.dtype) for a in (gq, gkv, small)]
        + [pltpu.SemaphoreType.DMA((3,))],
        compiler_params=pltpu.CompilerParams(vmem_limit_bytes=VMEM),
        name="finish",
    )(gq, gkv, small)


def local(q_in, k_in, v_in, short_weights, residues, log_decay, out_weight, grad_out):
    parts = mixer(
        q_in, k_in, v_in, short_weights, residues.T, log_decay.T, out_weight, grad_out
    )
    gq, gk, gv, short, res, dec = finish(*parts)
    return gq, gk, gv, short, res.T, dec.T


def solution(mesh):
    in_specs = (
        P("pos", "chan"),
        P("pos", "chan"),
        P("pos", "chan"),
        P(None, None, "chan"),
        P("chan", None),
        P("chan", None),
        P("chan", "pos"),
        P(("pos", "chan"), None),
    )
    out_specs = (
        P("pos", "chan"),
        P("pos", "chan"),
        P("pos", "chan"),
        P(None, None, "chan"),
        P("chan", None),
        P("chan", None),
    )
    return jax.shard_map(local, mesh=mesh, in_specs=in_specs, out_specs=out_specs, check_vma=False)
```
